256 devices in a mesh: sub: 64 (over z, y, x_hi), rng: 4 (over x_lo, core).
Axes of the slice: x: 4 (x_hi: 2, x_lo: 2; x = x_hi * 2 + x_lo), y: 4, z: 8, core: 2. Of those that a mesh axis runs over, the one named last changes fastest.
Arguments:
- images: bfloat16 [2, 128, 1024, 256], P(None, 'sub', 'rng'), may hold values from -6 to 6
- beam_index: int32 [2, 7680], replicated, may hold values from 0 to 2044, as said below
- range_shift: int32 [2, 7680], replicated, may hold values from -2 to 2
- tap_weights: bfloat16 [2, 4, 7680], replicated, may hold values from -2 to 2
- phase_base: float32 [2, 7680], replicated, may hold values from -3.140625 to 3.140625
- phase_slope: float32 [2, 7680], replicated, may hold values from -0.05 to 0.05
Outputs:
- final: bfloat16 [2, 64, 4, 32, 4096], P(None, 'sub', 'rng')
The draws below stay inside these ranges and needn't reach their ends.
Inputs may be any that keep to these rules, and one draw needn't show every extreme that they name: `beam_index`: for output beam j of a section whose input images have W beams, the entry lies within j // 2 - 3 to j // 2 - 1, clipped to 0 .. W - 4.
All inputs are finite; a program needn't handle non-finite values.
Results may differ from the reference program's by a relative error of at most 0.0064.
Values may be sent and summed in bfloat16 or wider, within the bound.
A program may use at most 64 MiB of HBM per device.

```python
import jax
import jax.numpy as jnp
from jax import lax

BEAMS = 256
SECTIONS = 4
TAPS = 4
SHIFT = 2
SUBS = 128
ROWS = 1024
FINAL_BEAMS = 4096
FINAL_ROWS = 32
TABLE_COLS = 7680
N_SUB = 64
N_RNG = 4


def draw_beam_index(key, part):
    key = jax.random.fold_in(key, 7)
    centres = []
    limits = []
    for section in range(SECTIONS):
        width = BEAMS * 2 ** section
        columns = jnp.arange(2 * width, dtype=jnp.int32)
        centres.append(columns // 2)
        limits.append(jnp.full((2 * width,), width - TAPS, jnp.int32))
    centre = jnp.concatenate(centres)
    limit = jnp.concatenate(limits)
    jitter = jax.random.randint(key, (2, TABLE_COLS), -3, 0).astype(jnp.int32)
    return jnp.clip(centre[None, :] + jitter, 0, limit[None, :]).astype(jnp.int32)


def plant(entries, stream_key, smallest, largest):
    longest = entries.shape.index(max(entries.shape))
    spots = []
    for shift in (0, 1):
        where = [jax.random.randint(jax.random.fold_in(stream_key, axis), (), 0, length) for axis, length in enumerate(entries.shape)]
        where[longest] = (where[longest] + shift) % entries.shape[longest]
        spots.append(tuple(where))
    return entries.at[spots[0]].set(smallest).at[spots[1]].set(largest)


def block_scale(rng, dims, pieces, low, high):
    def one(dim, blocks):
        steps = jax.random.uniform(jax.random.fold_in(jax.random.fold_in(rng, 6), dim), (blocks,), jnp.float32, low / len(pieces), high / len(pieces))
        return jnp.repeat(jnp.exp(steps), dims[dim] // blocks).reshape((-1,) + (1,) * (len(dims) - dim - 1))

    loudness = one(*pieces[0])
    for cut in pieces[1:]:
        loudness = loudness * one(*cut)
    return loudness


def scatter_about(stream_key, dims, scale, reach, split=(), held_as=jnp.bfloat16):
    factor_of = block_scale(stream_key, dims, split, -0.22, 0.18) if split else 1.0
    result = jax.random.normal(stream_key, dims, jnp.float32) * scale * factor_of
    return jnp.minimum(jnp.maximum(result, -reach), reach).astype(held_as)


def setup_inputs(seed: int = 0) -> dict:
    splits = jax.random.split(jax.random.key(seed), 7)
    images = scatter_about(splits[0], (2, SUBS, ROWS, BEAMS), 1.0, 6.0, ((1, 64), (2, 4)))
    beam_index = draw_beam_index(jax.random.fold_in(splits[6], 71), 0)
    range_shift = plant(jax.random.randint(splits[2], (2, TABLE_COLS), -SHIFT, SHIFT + 1), jax.random.fold_in(splits[2], 1), -SHIFT, SHIFT).astype(jnp.int32)
    tap_weights = scatter_about(splits[3], (2, TAPS, TABLE_COLS), 8 ** -0.5, 2.0)
    phase_base = jnp.clip(jax.random.uniform(splits[4], (2, TABLE_COLS), jnp.float32, -3.140625, 3.140625), -3.140625, 3.140625)
    phase_slope = jnp.clip(jax.random.uniform(splits[5], (2, TABLE_COLS), jnp.float32, -0.05, 0.05), -0.05, 0.05)
    return {"images": images, "beam_index": beam_index, "range_shift": range_shift, "tap_weights": tap_weights, "phase_base": phase_base, "phase_slope": phase_slope}


def child_term(child, index, shift, weights, base, slope):
    values = child.astype(jnp.float32)
    total = jnp.zeros((2, values.shape[1], index.shape[0]), jnp.float32)
    for tap in range(TAPS):
        picked = jnp.take(values, (index + tap).astype(jnp.int32), axis=2)
        total = total + picked * weights[tap].astype(jnp.float32)[None, None, :]
    padded = jnp.pad(total, ((0, 0), (SHIFT, SHIFT), (0, 0)))
    moved = jnp.zeros_like(total)
    for offset in range(-SHIFT, SHIFT + 1):
        part = padded[:, SHIFT + offset:SHIFT + offset + ROWS, :]
        moved = moved + jnp.where((shift == offset)[None, None, :], part, jnp.float32(0.0))
    rows_f = jnp.arange(ROWS, dtype=jnp.float32)[:, None]
    theta = base[None, :] + slope[None, :] * rows_f
    cosine = jnp.cos(theta)
    sine = jnp.sin(theta)
    real = cosine * moved[0] - sine * moved[1]
    imag = sine * moved[0] + cosine * moved[1]
    return jnp.stack([real, imag])


def reference(images, beam_index, range_shift, tap_weights, phase_base, phase_slope):
    stack = jnp.transpose(images, (1, 0, 2, 3))
    for section in range(SECTIONS):
        if section == 0:
            firsts = stack[0::2]
            seconds = stack[1::2]
        else:
            count = stack.shape[0] // 2
            firsts = stack[:count]
            seconds = stack[count:]
        width = stack.shape[3]
        start = BEAMS * (2 ** (section + 1) - 2)
        stop = start + 2 * width
        index = beam_index[:, start:stop]
        shift = range_shift[:, start:stop]
        weights = tap_weights[:, :, start:stop]
        base = phase_base[:, start:stop]
        slope = phase_slope[:, start:stop]

        def merge_pair(items, index=index, shift=shift, weights=weights, base=base, slope=slope):
            one = child_term(items[0], index[0], shift[0], weights[0], base[0], slope[0])
            two = child_term(items[1], index[1], shift[1], weights[1], base[1], slope[1])
            return (one + two).astype(jnp.bfloat16)

        stack = lax.map(merge_pair, (firsts, seconds))
    groups = N_SUB // 8
    shaped = stack.reshape(groups, 2, N_RNG, 8, FINAL_ROWS, FINAL_BEAMS)
    shaped = jnp.transpose(shaped, (1, 3, 0, 2, 4, 5))
    return shaped.reshape(2, N_SUB, N_RNG, FINAL_ROWS, FINAL_BEAMS)
```

```python
import functools

import jax
import jax.numpy as jnp
from jax import lax
from jax.experimental import pallas as pl
from jax.experimental.pallas import tpu as pltpu
from jax.sharding import PartitionSpec as P

MESH = pl.DeviceIdType.MESH
BF16 = jnp.bfloat16
F32 = jnp.float32
CHIPS = 8
COLUMN = 8
STRIPS = 4
STRIP = 256
TILE = 32
HALO = 8
BLOCK = TILE + 2 * HALO
BEAMS = 256
LANES = 128
TAPS = 4
SHIFT = 2
TILES = (4, 10, 18, 34)
FIRST = (0, 4, 14, 32)
TABLE = (0, 4, 12, 28)
BAND_ROWS = 96


def build_tables(z, q, idx, shf, wts, base, slope, band, cos_t, sin_t):
    start = (q * STRIP + z * TILE - HALO).astype(F32)
    iota8 = lax.broadcasted_iota(jnp.int32, (8, LANES), 0).astype(F32)
    iota_k = lax.broadcasted_iota(jnp.int32, (BAND_ROWS, LANES), 0)

    def one(child, tile, col, origin, offset):
        band[child, tile] = jnp.zeros((BEAMS, LANES), BF16)
        cols = pl.ds(col, LANES)
        first = idx[child : child + 1, cols] - (origin + offset)
        weights = wts[child, :, cols].astype(F32)
        patch = jnp.zeros((BAND_ROWS, LANES), F32)
        for tap in range(TAPS):
            patch = jnp.where(iota_k == first + tap, weights[tap : tap + 1, :], patch)
        if not isinstance(offset, int):
            offset = pl.multiple_of(offset, 16)
        band[child, tile, pl.ds(offset, BAND_ROWS), :] = patch.astype(BF16)
        rate = slope[child : child + 1, cols]
        theta = base[child : child + 1, cols] + rate * (start + iota8)
        c, s = jnp.cos(theta), jnp.sin(theta)
        turn = jnp.broadcast_to(rate * 8.0, (8, LANES))
        c8, s8 = jnp.cos(turn), jnp.sin(turn)
        for step in range(BLOCK // 8):
            cos_t[child, tile, step * 8 : step * 8 + 8, :] = c
            sin_t[child, tile, step * 8 : step * 8 + 8, :] = s
            c, s = c * c8 - s * s8, s * c8 + c * s8

    for child in range(2):
        for tile in range(TILES[0]):
            one(child, tile, tile * LANES, 0, (0, 48, 112, 160)[tile])
    for section in range(1, 4):
        last = TILES[section] - 1
        for child in range(2):
            for pad in (0, last):
                band[child, FIRST[section] + pad] = jnp.zeros((BEAMS, LANES), BF16)
                cos_t[child, FIRST[section] + pad] = jnp.zeros((BLOCK, LANES), F32)
                sin_t[child, FIRST[section] + pad] = jnp.zeros((BLOCK, LANES), F32)

        def body(tile, carry, section=section):
            block, side = tile // 2, tile % 2
            for child in range(2):
                one(
                    child,
                    FIRST[section] + tile,
                    pl.multiple_of((TABLE[section] + tile - 1) * LANES, LANES),
                    LANES * (block - 1),
                    48 + 64 * side,
                )
            return carry

        lax.fori_loop(1, last, body, 0)


def masks_of(shf, col):
    found = []
    for child in range(2):
        row = jnp.broadcast_to(shf[child : child + 1, pl.ds(col, LANES)], (16, LANES))
        found.append({o: row == o for o in (-2, -1, 1, 2)})
    return found


def merged_rows(v, slot, masks, cos_t, sin_t, tile, row):
    moved = []
    for child in range(2):
        for plane in range(2):
            at = HALO + row
            u = v[child, plane, slot, at : at + 16, :]
            for o in (-2, -1, 1, 2):
                u = jnp.where(masks[child][o], v[child, plane, slot, at + o : at + o + 16, :], u)
            moved.append(u)
    c0, s0 = cos_t[0, tile, row : row + 16, :], sin_t[0, tile, row : row + 16, :]
    c1, s1 = cos_t[1, tile, row : row + 16, :], sin_t[1, tile, row : row + 16, :]
    real = (c0 * moved[0] - s0 * moved[1]) + (c1 * moved[2] - s1 * moved[3])
    imag = (s0 * moved[0] + c0 * moved[1]) + (s1 * moved[2] + c1 * moved[3])
    return real, imag


def section_zero(image, low, high, recv, shf, band, cos_t, sin_t, v, out):
    iota = lax.broadcasted_iota(jnp.int32, (16, LANES), 0)
    for child in range(2):
        lhs = recv[image, :, child].reshape(2 * BLOCK, BEAMS)
        rhs = jnp.concatenate([band[child, t] for t in range(4)], axis=1)
        product = jnp.dot(lhs, rhs, preferred_element_type=F32)
        for plane in range(2):
            for t in range(4):
                v[child, plane, t, HALO : HALO + BLOCK, :] = product[
                    plane * BLOCK : (plane + 1) * BLOCK, t * LANES : (t + 1) * LANES
                ]
    for t in range(4):
        masks = masks_of(shf, t * LANES)
        for row in range(0, BLOCK, 16):
            real, imag = merged_rows(v, t, masks, cos_t, sin_t, t, row)
            inside = (iota + row >= low) & (iota + row < high)
            cols = slice((t + 1) * LANES, (t + 2) * LANES)
            out[0, image, row : row + 16, cols] = jnp.where(inside, real, 0.0).astype(BF16)
            out[1, image, row : row + 16, cols] = jnp.where(inside, imag, 0.0).astype(BF16)


def section_later(section, low, high, source, shf, band, cos_t, sin_t, v, out):
    images = 8 >> section
    tiles = TILES[section]
    iota = lax.broadcasted_iota(jnp.int32, (16, LANES), 0)

    def block_body(block, carry):
        window = pl.ds(pl.multiple_of(block * LANES, LANES), BEAMS)
        for child in range(2):
            lhs = source[:, child * images : (child + 1) * images, :, window]
            lhs = lhs.reshape(2 * images * BLOCK, BEAMS)
            pair = FIRST[section] + 2 * block
            rhs = jnp.concatenate([band[child, pair], band[child, pair + 1]], axis=1)
            product = jnp.dot(lhs, rhs, preferred_element_type=F32)
            for plane in range(2):
                for image in range(images):
                    at = (plane * images + image) * BLOCK
                    for side in range(2):
                        v[child, plane, 2 * image + side, HALO : HALO + BLOCK, :] = product[
                            at : at + BLOCK, side * LANES : (side + 1) * LANES
                        ]
        for side in range(2):
            tile = 2 * block + side
            known = jnp.clip(tile - 1, 0, tiles - 3)
            masks = masks_of(shf, pl.multiple_of((TABLE[section] + known) * LANES, LANES))
            cols = pl.ds(pl.multiple_of(tile * LANES, LANES), LANES)
            for image in range(images):
                if section < 3:
                    for row in range(0, BLOCK, 16):
                        real, imag = merged_rows(
                            v, 2 * image + side, masks, cos_t, sin_t, FIRST[section] + tile, row
                        )
                        inside = (iota + row >= low) & (iota + row < high)
                        out[0, image, row : row + 16, cols] = jnp.where(inside, real, 0.0).astype(BF16)
                        out[1, image, row : row + 16, cols] = jnp.where(inside, imag, 0.0).astype(BF16)
                else:
                    for row in range(0, TILE, 16):
                        real, imag = merged_rows(
                            v, side, masks, cos_t, sin_t, FIRST[section] + tile, row + HALO
                        )
                        out[0, row : row + 16, cols] = real.astype(BF16)
                        out[1, row : row + 16, cols] = imag.astype(BF16)
        return carry

    lax.fori_loop(0, tiles // 2, block_body, 0)


def kernel(
    images, idx, shf, wts, base, slope, final,
    xin, send, recv, hsend, hrecv, band, cos_t, sin_t, s1, s2, s3, outs, v,
    local_sem, send_sem, recv_sem, hsend_sem, hrecv_sem, comm=True, place=None,
):
    if comm:
        sub, q = lax.axis_index("sub"), lax.axis_index("rng")
        z, lane = sub // COLUMN, sub % COLUMN
    else:
        z, q = place
        z, q = jnp.int32(z), jnp.int32(q)

    def device(zz, qq):
        return (zz * COLUMN + lane, qq)

    if comm:
        barrier = pltpu.get_barrier_semaphore()
        for step in range(1, CHIPS):
            pl.semaphore_signal(
                barrier, inc=1, device_id=device((z + step) % CHIPS, q), device_id_type=MESH
            )

        @pl.when((z == 0) & (q > 0))
        def _():
            for other in range(CHIPS):
                pl.semaphore_signal(
                    barrier, inc=1, device_id=device(other, q - 1), device_id_type=MESH
                )

        @pl.when((z == CHIPS - 1) & (q < STRIPS - 1))
        def _():
            for other in range(CHIPS):
                pl.semaphore_signal(
                    barrier, inc=1, device_id=device(other, q + 1), device_id_type=MESH
                )

        load = pltpu.make_async_copy(images, xin, local_sem)
        load.start()
        load.wait()
        send[0, :, :, 0:HALO, :] = jnp.zeros((2, 2, HALO, BEAMS), BF16)
        send[CHIPS - 1, :, :, BLOCK - HALO :, :] = jnp.zeros((2, 2, HALO, BEAMS), BF16)
        for to in range(CHIPS):
            begin, end = max(TILE * to - HALO, 0), min(TILE * to + TILE + HALO, STRIP)
            at = begin - (TILE * to - HALO)
            send[to, :, :, at : at + end - begin, :] = xin[:, :, begin:end, :]
        for image in range(2):
            rows = slice(image * HALO, (image + 1) * HALO)
            hsend[0, :, rows, :] = xin[:, image, STRIP - HALO :, :]
            hsend[1, :, rows, :] = xin[:, image, 0:HALO, :]
        peers = CHIPS - 1 + (q > 0).astype(jnp.int32) + (q < STRIPS - 1).astype(jnp.int32)
        pl.semaphore_wait(barrier, peers)

        def block_copy(step):
            return pltpu.make_async_remote_copy(
                src_ref=send.at[(z + step) % CHIPS],
                dst_ref=recv.at[z],
                send_sem=send_sem.at[step],
                recv_sem=recv_sem.at[step],
                device_id=device((z + step) % CHIPS, q),
                device_id_type=MESH,
            )

        def halo_copy(side):
            return pltpu.make_async_remote_copy(
                src_ref=hsend.at[side],
                dst_ref=hrecv.at[z],
                send_sem=hsend_sem.at[side],
                recv_sem=hrecv_sem.at[z],
                device_id=device(0, q + 1) if side == 0 else device(CHIPS - 1, q - 1),
                device_id_type=MESH,
            )

        @pl.when(q < STRIPS - 1)
        def _():
            halo_copy(0).start()

        @pl.when(q > 0)
        def _():
            halo_copy(1).start()

        for step in (1, 7, 2, 6, 3, 5, 4):
            block_copy(step).start()
        recv[z] = send[z]
    else:
        load = pltpu.make_async_copy(images, recv, local_sem)
        load.start()
        load.wait()

    build_tables(z, q, idx, shf, wts, base, slope, band, cos_t, sin_t)
    for ref, width in ((s1, 512), (s2, 1024), (s3, 2048)):
        lead = ref.shape[:-1]
        ref[..., 0:LANES] = jnp.zeros(lead + (LANES,), BF16)
        ref[..., LANES + width :] = jnp.zeros(lead + (LANES,), BF16)

    low = jnp.where((z == 0) & (q == 0), HALO, 0)
    high = jnp.where((z == CHIPS - 1) & (q == STRIPS - 1), BLOCK - HALO, BLOCK)

    def arrival(turn, carry):
        step = jnp.where(turn % 2 == 1, (turn + 1) // 2, (CHIPS - turn // 2) % CHIPS)
        image = (z + CHIPS - step) % CHIPS
        if comm:

            @pl.when(turn > 0)
            def _():
                pltpu.make_async_remote_copy(
                    src_ref=send.at[image],
                    dst_ref=recv.at[image],
                    send_sem=send_sem.at[step],
                    recv_sem=recv_sem.at[step],
                    device_id=device(image, q),
                    device_id_type=MESH,
                ).wait_recv()

            def take(rows):
                pltpu.make_async_remote_copy(
                    src_ref=hsend.at[0],
                    dst_ref=hrecv.at[image],
                    send_sem=hsend_sem.at[0],
                    recv_sem=hrecv_sem.at[image],
                    device_id=device(image, q),
                    device_id_type=MESH,
                ).wait_recv()
                for part in range(2):
                    recv[image, :, part, rows, :] = hrecv[
                        image, :, part * HALO : (part + 1) * HALO, :
                    ]

            @pl.when((z == 0) & (q > 0))
            def _():
                take(slice(0, HALO))

            @pl.when((z == CHIPS - 1) & (q < STRIPS - 1))
            def _():
                take(slice(BLOCK - HALO, BLOCK))

        section_zero(image, low, high, recv, shf, band, cos_t, sin_t, v, s1)
        return carry

    lax.fori_loop(0, CHIPS, arrival, 0)
    section_later(1, low, high, s1, shf, band, cos_t, sin_t, v, s2)
    section_later(2, low, high, s2, shf, band, cos_t, sin_t, v, s3)
    section_later(3, low, high, s3, shf, band, cos_t, sin_t, v, outs)

    store = pltpu.make_async_copy(outs.at[:, :, pl.ds(LANES, 4096)], final, local_sem)
    store.start()
    if comm:
        for step in range(1, CHIPS):
            block_copy(step).wait_send()

        @pl.when(q < STRIPS - 1)
        def _():
            halo_copy(0).wait_send()

        @pl.when(q > 0)
        def _():
            halo_copy(1).wait_send()

    store.wait()


def call(images, tables, comm=True, place=None):
    vmem = pl.BlockSpec(memory_space=pltpu.VMEM)
    anywhere = pl.BlockSpec(memory_space=pl.ANY)
    dma = pltpu.SemaphoreType.DMA
    tiles = sum(TILES)
    params = dict(vmem_limit_bytes=48 * 2**20, has_side_effects=True)
    if comm:
        params["collective_id"] = 0
    return pl.pallas_call(
        functools.partial(kernel, comm=comm, place=place),
        out_shape=jax.ShapeDtypeStruct((2, TILE, 4096), BF16),
        in_specs=[anywhere] + [vmem] * 5,
        out_specs=anywhere,
        scratch_shapes=[
            pltpu.VMEM((2, 2, STRIP, BEAMS), BF16),
            pltpu.VMEM((CHIPS, 2, 2, BLOCK, BEAMS), BF16),
            pltpu.VMEM((CHIPS, 2, 2, BLOCK, BEAMS), BF16),
            pltpu.VMEM((2, 2, 2 * HALO, BEAMS), BF16),
            pltpu.VMEM((CHIPS, 2, 2 * HALO, BEAMS), BF16),
            pltpu.VMEM((2, tiles, BEAMS, LANES), BF16),
            pltpu.VMEM((2, tiles, BLOCK, LANES), F32),
            pltpu.VMEM((2, tiles, BLOCK, LANES), F32),
            pltpu.VMEM((2, 8, BLOCK, 512 + 2 * LANES), BF16),
            pltpu.VMEM((2, 4, BLOCK, 1024 + 2 * LANES), BF16),
            pltpu.VMEM((2, 2, BLOCK, 2048 + 2 * LANES), BF16),
            pltpu.VMEM((2, TILE, 4096 + 2 * LANES), BF16),
            pltpu.VMEM((2, 2, 8, BLOCK + 2 * HALO, LANES), F32),
            dma,
            dma((CHIPS,)),
            dma((CHIPS,)),
            dma((2,)),
            dma((CHIPS,)),
        ],
        compiler_params=pltpu.CompilerParams(**params),
    )(images, *tables)


def local(images, *tables):
    return call(images[:, :], tables).reshape(2, 1, 1, TILE, 4096)


def solution(mesh):
    in_specs = (P(None, "sub", "rng", None), P(), P(), P(), P(), P())
    out_specs = P(None, "sub", "rng", None, None)
    return jax.shard_map(local, mesh=mesh, in_specs=in_specs, out_specs=out_specs, check_vma=False)
```

```python
import functools

import jax
import jax.numpy as jnp
from jax import lax
from jax.experimental import pallas as pl
from jax.experimental.pallas import tpu as pltpu
from jax.sharding import PartitionSpec as P

MESH = pl.DeviceIdType.MESH
BF16 = jnp.bfloat16
F32 = jnp.float32
CHIPS = 8
COLUMN = 8
STRIPS = 4
STRIP = 256
TILE = 32
HALO = 8
BLOCK = TILE + 2 * HALO
GROUP = 8
BEAMS = 256
LANES = 128
TAPS = 4
SHIFT = 2
TILES = (4, 8, 16, 32)
FIRST = (0, 4, 12, 28)
ROWS = (48, 40, 40, 32)
BASE = (-6, -4, -2, 0)
BAND_ROWS = 96
SLOTS = 4


def build_tables(z, q, idx, shf, wts, base, slope, band, cos_t, sin_t):
    origin_row = q * STRIP + z * TILE
    iota8 = lax.broadcasted_iota(jnp.int32, (8, LANES), 0)
    iota_k = lax.broadcasted_iota(jnp.int32, (BAND_ROWS, LANES), 0)

    def one(section, child, tile, origin, offset):
        cols = pl.ds(pl.multiple_of(tile * LANES, LANES), LANES)
        band[child, tile] = jnp.zeros((BEAMS, LANES), BF16)
        first = idx[child : child + 1, cols] - (origin + offset)
        weights = wts[child, :, cols].astype(F32)
        patch = jnp.zeros((BAND_ROWS, LANES), F32)
        for tap in range(TAPS):
            patch = jnp.where(iota_k == first + tap, weights[tap : tap + 1, :], patch)
        if not isinstance(offset, int):
            offset = pl.multiple_of(offset, 16)
        band[child, tile, pl.ds(offset, BAND_ROWS), :] = patch.astype(BF16)
        rate = slope[child : child + 1, cols]
        rows = (iota8 + (origin_row + BASE[section])).astype(F32)
        theta = base[child : child + 1, cols] + rate * rows
        c, s = jnp.cos(theta), jnp.sin(theta)
        turn = jnp.broadcast_to(rate * 8.0, (8, LANES))
        c8, s8 = jnp.cos(turn), jnp.sin(turn)
        for step in range(ROWS[section] // 8):
            cos_t[child, tile, step * 8 : step * 8 + 8, :] = c
            sin_t[child, tile, step * 8 : step * 8 + 8, :] = s
            c, s = c * c8 - s * s8, s * c8 + c * s8

    for child in range(2):
        for tile in range(TILES[0]):
            one(0, child, tile, 0, (0, 48, 112, 160)[tile])
    for section in range(1, 4):
        tiles = TILES[section]

        def body(tile, carry, section=section, tiles=tiles):
            block = (tile + 1) // 2
            side = (tile + 1) % 2
            for child in range(2):
                one(section, child, FIRST[section] + tile, LANES * (block - 1), 48 + 64 * side)
            return carry

        lax.fori_loop(0, tiles, body, 0)


def masks_of(shf, tile):
    found = []
    for child in range(2):
        cols = pl.ds(pl.multiple_of(tile * LANES, LANES), LANES)
        row = jnp.broadcast_to(shf[child : child + 1, cols], (16, LANES))
        found.append({o: row == o for o in (-2, -1, 1, 2)})
    return found


def merged_rows(v, slot, masks, cos_t, sin_t, tile, row, count):
    moved = []
    for child in range(2):
        for plane in range(2):
            at = row + SHIFT
            u = v[(*slot, child, plane, slice(at, at + count), slice(None))]
            for o in (-2, -1, 1, 2):
                other = v[(*slot, child, plane, slice(at + o, at + o + count), slice(None))]
                u = jnp.where(masks[child][o][:count], other, u)
            moved.append(u)
    rows = slice(row, row + count)
    c0, s0 = cos_t[0, tile, rows, :], sin_t[0, tile, rows, :]
    c1, s1 = cos_t[1, tile, rows, :], sin_t[1, tile, rows, :]
    real = (c0 * moved[0] - s0 * moved[1]) + (c1 * moved[2] - s1 * moved[3])
    imag = (s0 * moved[0] + c0 * moved[1]) + (s1 * moved[2] + c1 * moved[3])
    return real, imag


def combine(section, row0, v, slot, masks, cos_t, sin_t, tile, store):
    rows = ROWS[section]
    for row in range(0, rows, 16):
        count = min(16, rows - row)
        parts = merged_rows(v, slot, masks, cos_t, sin_t, tile, row, count)
        if section < 3 and row != 16:
            bins = lax.broadcasted_iota(jnp.int32, (count, LANES), 0) + (row0 + row + BASE[section])
            inside = (bins >= 0) & (bins < STRIPS * STRIP)
            parts = [jnp.where(inside, part, 0.0) for part in parts]
        if count < 16:
            rest = jnp.zeros((16 - count, LANES), F32)
            parts = [jnp.concatenate([part, rest], axis=0) for part in parts]
        for plane in range(2):
            store(plane, row, parts[plane].astype(BF16))


def section_zero(image, row0, recv, shf, band, cos_t, sin_t, v, out):
    for child in range(2):
        lhs = recv[image, :, child, 1 : 1 + BLOCK // GROUP].reshape(2 * BLOCK, BEAMS)
        rhs = jnp.concatenate([band[child, t] for t in range(4)], axis=1)
        product = jnp.dot(lhs, rhs, preferred_element_type=F32)
        for plane in range(2):
            for t in range(4):
                v[0, t, child, plane, 0:BLOCK, :] = product[
                    plane * BLOCK : (plane + 1) * BLOCK, t * LANES : (t + 1) * LANES
                ]
    for t in range(4):

        def store(plane, row, value, t=t):
            out[plane, image, row : row + 16, (t + 1) * LANES : (t + 2) * LANES] = value
            if t == 3:
                out[plane, image, row : row + 16, 0:LANES] = value

        combine(0, row0, v, (0, t), masks_of(shf, t), cos_t, sin_t, t, store)


def section_later(section, row0, source, shf, band, cos_t, sin_t, v, out):
    images = 8 >> section
    tiles = TILES[section]

    def tiles_of(block):
        return (lax.rem(2 * block + tiles - 1, tiles), 2 * block)

    def multiply(slot, block):
        window = pl.ds(pl.multiple_of(block * LANES, LANES), BEAMS)
        here = tiles_of(block)
        for child in range(2):
            lhs = source[:, child * images : (child + 1) * images, :, window]
            lhs = lhs.reshape(2 * images * BLOCK, BEAMS)
            rhs = jnp.concatenate([band[child, FIRST[section] + t] for t in here], axis=1)
            product = jnp.dot(lhs, rhs, preferred_element_type=F32)
            for plane in range(2):
                for image in range(images):
                    at = (plane * images + image) * BLOCK
                    for side in range(2):
                        v[slot, 2 * image + side, child, plane, 0:BLOCK, :] = product[
                            at : at + BLOCK, side * LANES : (side + 1) * LANES
                        ]

    def finish(slot, block):
        for side, t in enumerate(tiles_of(block)):
            tile = FIRST[section] + t
            masks = masks_of(shf, tile)
            for image in range(images):

                def store(plane, row, value, side=side, t=t, image=image):
                    if section == 3:
                        cols = pl.ds(pl.multiple_of(t * LANES, LANES), LANES)
                        out[plane, row : row + 16, cols] = value
                        return
                    cols = pl.ds(pl.multiple_of((t + 1) * LANES, LANES), LANES)
                    out[plane, image, row : row + 16, cols] = value
                    if side == 0 and isinstance(block, int) and block == 0:
                        out[plane, image, row : row + 16, 0:LANES] = value

                combine(section, row0, v, (slot, 2 * image + side), masks, cos_t, sin_t, tile, store)

    def step(first):
        multiply(0, first)
        for slot in range(1, SLOTS):
            multiply(slot, first + slot)
            finish(slot - 1, first + slot - 1)
        finish(SLOTS - 1, first + SLOTS - 1)

    def body(turn, carry):
        step(turn * SLOTS)
        return carry

    lax.fori_loop(0, tiles // 2 // SLOTS, body, 0)
    if section < 3:
        out[:, :, :, 0:LANES] = out[:, :, :, tiles * LANES : (tiles + 1) * LANES]


def kernel(
    images, idx_h, shf_h, wts_h, base_h, slope_h, final,
    recv, idx, shf, wts, base, slope, band, cos_t, sin_t, s1, s2, s3, v,
    local_sem, table_sem, send_sem, recv_sem, hsend_sem, hrecv_sem, comm=True, place=None,
):
    if comm:
        sub, q = lax.axis_index("sub"), lax.axis_index("rng")
        z, lane = sub // COLUMN, sub % COLUMN
    else:
        z, q = jnp.int32(place[0]), jnp.int32(place[1])

    def device(zz, qq):
        return (zz * COLUMN + lane, qq)

    if comm:
        barrier = pltpu.get_barrier_semaphore()
        for step in range(1, CHIPS):
            pl.semaphore_signal(
                barrier, inc=1, device_id=device((z + step) % CHIPS, q), device_id_type=MESH
            )

        @pl.when((z == 0) & (q > 0))
        def _():
            for other in range(CHIPS):
                pl.semaphore_signal(
                    barrier, inc=1, device_id=device(other, q - 1), device_id_type=MESH
                )

        @pl.when((z == CHIPS - 1) & (q < STRIPS - 1))
        def _():
            for other in range(CHIPS):
                pl.semaphore_signal(
                    barrier, inc=1, device_id=device(other, q + 1), device_id_type=MESH
                )

    fetches = [
        pltpu.make_async_copy(src, dst, table_sem.at[i])
        for i, (src, dst) in enumerate(
            ((idx_h, idx), (shf_h, shf), (wts_h, wts), (base_h, base), (slope_h, slope))
        )
    ]
    for fetch in fetches:
        fetch.start()

    groups = BLOCK // GROUP

    def spans(to):
        wanted = to * (TILE // GROUP) - 1
        begin = jnp.clip(wanted, 0, STRIP // GROUP - groups)
        return pl.ds(begin, groups), pl.ds(1 + begin - wanted, groups)

    if comm:
        src, dst = spans(z)
        own = pltpu.make_async_copy(
            images.at[:, :, src], recv.at[z, :, :, dst], local_sem
        )
        own.start()
        peers = CHIPS - 1 + (q > 0).astype(jnp.int32) + (q < STRIPS - 1).astype(jnp.int32)
        pl.semaphore_wait(barrier, peers)

        def block_copy(step):
            to = (z + step) % CHIPS
            src, dst = spans(to)
            return pltpu.make_async_remote_copy(
                src_ref=images.at[:, :, src],
                dst_ref=recv.at[z, :, :, dst],
                send_sem=send_sem.at[step],
                recv_sem=recv_sem.at[step],
                device_id=device(to, q),
                device_id_type=MESH,
            )

        def halo_copy(side):
            src, dst = ((STRIP // GROUP - 1, 1), (0, groups))[side]
            return pltpu.make_async_remote_copy(
                src_ref=images.at[:, :, src],
                dst_ref=recv.at[z, :, :, dst],
                send_sem=hsend_sem.at[side],
                recv_sem=hrecv_sem.at[z],
                device_id=device(0, q + 1) if side == 0 else device(CHIPS - 1, q - 1),
                device_id_type=MESH,
            )

        for step in (1, 7, 2, 6, 3, 5, 4):
            block_copy(step).start()

        @pl.when(q < STRIPS - 1)
        def _():
            halo_copy(0).start()

        @pl.when(q > 0)
        def _():
            halo_copy(1).start()

        @pl.when((z == 0) & (q == 0))
        def _():
            recv[:, :, :, 1] = jnp.zeros((CHIPS, 2, 2, GROUP, BEAMS), BF16)

        @pl.when((z == CHIPS - 1) & (q == STRIPS - 1))
        def _():
            recv[:, :, :, groups] = jnp.zeros((CHIPS, 2, 2, GROUP, BEAMS), BF16)
    else:
        own = pltpu.make_async_copy(images, recv.at[:, :, :, pl.ds(1, groups)], local_sem)
        own.start()

    for fetch in fetches:
        fetch.wait()
    build_tables(z, q, idx, shf, wts, base, slope, band, cos_t, sin_t)
    own.wait()
    row0 = q * STRIP + z * TILE

    def arrival(turn, carry):
        step = jnp.where(turn % 2 == 1, (turn + 1) // 2, (CHIPS - turn // 2) % CHIPS)
        image = (z + CHIPS - step) % CHIPS
        if comm:

            @pl.when(turn > 0)
            def _():
                src, dst = spans(z)
                pltpu.make_async_remote_copy(
                    src_ref=images.at[:, :, src],
                    dst_ref=recv.at[image, :, :, dst],
                    send_sem=send_sem.at[step],
                    recv_sem=recv_sem.at[step],
                    device_id=device(image, q),
                    device_id_type=MESH,
                ).wait_recv()

            def halo_wait(at):
                pltpu.make_async_remote_copy(
                    src_ref=images.at[:, :, 0],
                    dst_ref=recv.at[image, :, :, at],
                    send_sem=hsend_sem.at[0],
                    recv_sem=hrecv_sem.at[image],
                    device_id=device(image, q),
                    device_id_type=MESH,
                ).wait_recv()

            @pl.when((z == 0) & (q > 0))
            def _():
                halo_wait(1)

            @pl.when((z == CHIPS - 1) & (q < STRIPS - 1))
            def _():
                halo_wait(groups)

        section_zero(image, row0, recv, shf, band, cos_t, sin_t, v, s1)
        return carry

    lax.fori_loop(0, CHIPS, arrival, 0)
    section_later(1, row0, s1, shf, band, cos_t, sin_t, v, s2)
    section_later(2, row0, s2, shf, band, cos_t, sin_t, v, s3)
    section_later(3, row0, s3, shf, band, cos_t, sin_t, v, final)

    if comm:
        for step in range(1, CHIPS):
            block_copy(step).wait_send()

        @pl.when(q < STRIPS - 1)
        def _():
            halo_copy(0).wait_send()

        @pl.when(q > 0)
        def _():
            halo_copy(1).wait_send()


def call(images, tables, comm=True, place=None):
    vmem = pl.BlockSpec(memory_space=pltpu.VMEM)
    hbm = pl.BlockSpec(memory_space=pltpu.HBM)
    dma = pltpu.SemaphoreType.DMA
    tiles = sum(TILES)
    params = dict(vmem_limit_bytes=62 * 2**20, has_side_effects=True)
    if comm:
        params["collective_id"] = 0
    return pl.pallas_call(
        functools.partial(kernel, comm=comm, place=place),
        out_shape=jax.ShapeDtypeStruct((2, TILE, 4096), BF16),
        in_specs=[hbm] * 6,
        out_specs=vmem,
        scratch_shapes=[
            pltpu.VMEM((CHIPS, 2, 2, BLOCK // GROUP + 2, GROUP, BEAMS), BF16),
            *[pltpu.VMEM(table.shape, table.dtype) for table in tables],
            pltpu.VMEM((2, tiles, BEAMS, LANES), BF16),
            pltpu.VMEM((2, tiles, BLOCK, LANES), F32),
            pltpu.VMEM((2, tiles, BLOCK, LANES), F32),
            pltpu.VMEM((2, 8, BLOCK, 512 + LANES), BF16),
            pltpu.VMEM((2, 4, BLOCK, 1024 + LANES), BF16),
            pltpu.VMEM((2, 2, BLOCK, 2048 + LANES), BF16),
            pltpu.VMEM((SLOTS, 8, 2, 2, BLOCK + GROUP, LANES), F32),
            dma,
            dma((len(tables),)),
            dma((CHIPS,)),
            dma((CHIPS,)),
            dma((2,)),
            dma((CHIPS,)),
        ],
        compiler_params=pltpu.CompilerParams(**params),
    )(images, *tables)


def local(images, *tables):
    grouped = images.reshape(2, 2, STRIP // GROUP, GROUP, BEAMS)
    return call(grouped, tables).reshape(2, 1, 1, TILE, 4096)


def solution(mesh):
    in_specs = (P(None, "sub", "rng", None), P(), P(), P(), P(), P())
    out_specs = P(None, "sub", "rng", None, None)
    return jax.shard_map(local, mesh=mesh, in_specs=in_specs, out_specs=out_specs, check_vma=False)
```

```python
import functools

import jax
import jax.numpy as jnp
from jax import lax
from jax.experimental import pallas as pl
from jax.experimental.pallas import tpu as pltpu
from jax.sharding import PartitionSpec as P

MESH = pl.DeviceIdType.MESH
BF16 = jnp.bfloat16
F32 = jnp.float32
CHIPS = 8
COLUMN = 8
STRIPS = 4
STRIP = 256
TILE = 32
HALO = 8
BLOCK = TILE + 2 * HALO
GROUP = 8
BEAMS = 256
LANES = 128
TAPS = 4
SHIFT = 2
TILES = (4, 8, 16, 32)
FIRST = (0, 4, 12, 28)
ROWS = (48, 40, 40, 32)
BASE = (-6, -4, -2, 0)
BAND_ROWS = 96
STEPS = (1, 7, 2, 6, 3, 5)
SLOTS = 4


def build_tables(z, q, idx, shf, wts, base, slope, band, cos_t, sin_t, sections):
    origin_row = q * STRIP + z * TILE
    iota8 = lax.broadcasted_iota(jnp.int32, (8, LANES), 0)
    iota_k = lax.broadcasted_iota(jnp.int32, (BAND_ROWS, LANES), 0)

    def one(section, child, tile, origin, offset):
        cols = pl.ds(pl.multiple_of(tile * LANES, LANES), LANES)
        band[child, tile] = jnp.zeros((BEAMS, LANES), BF16)
        first = idx[child : child + 1, cols] - (origin + offset)
        weights = wts[child, :, cols].astype(F32)
        patch = jnp.zeros((BAND_ROWS, LANES), F32)
        for tap in range(TAPS):
            patch = jnp.where(iota_k == first + tap, weights[tap : tap + 1, :], patch)
        if not isinstance(offset, int):
            offset = pl.multiple_of(offset, 16)
        band[child, tile, pl.ds(offset, BAND_ROWS), :] = patch.astype(BF16)
        rate = slope[child : child + 1, cols]
        rows = (iota8 + (origin_row + BASE[section])).astype(F32)
        theta = base[child : child + 1, cols] + rate * rows
        c, s = jnp.cos(theta), jnp.sin(theta)
        turn = jnp.broadcast_to(rate * 8.0, (8, LANES))
        c8, s8 = jnp.cos(turn), jnp.sin(turn)
        for step in range(ROWS[section] // 8):
            cos_t[child, tile, step * 8 : step * 8 + 8, :] = c
            sin_t[child, tile, step * 8 : step * 8 + 8, :] = s
            c, s = c * c8 - s * s8, s * c8 + c * s8

    for child in range(2 if 0 in sections else 0):
        for tile in range(TILES[0]):
            one(0, child, tile, 0, (0, 48, 112, 160)[tile])
    for section in sections:
        if section == 0:
            continue
        tiles = TILES[section]

        def body(tile, carry, section=section, tiles=tiles):
            block = (tile + 1) // 2
            side = (tile + 1) % 2
            for child in range(2):
                one(section, child, FIRST[section] + tile, LANES * (block - 1), 48 + 64 * side)
            return carry

        lax.fori_loop(0, tiles, body, 0)


def masks_of(shf, tile):
    found = []
    for child in range(2):
        cols = pl.ds(pl.multiple_of(tile * LANES, LANES), LANES)
        row = jnp.broadcast_to(shf[child : child + 1, cols], (16, LANES))
        found.append({o: row == o for o in (-2, -1, 1, 2)})
    return found


def merged_rows(v, slot, masks, cos_t, sin_t, tile, row, count):
    moved = []
    for child in range(2):
        for plane in range(2):
            at = row + SHIFT
            u = v[(*slot, child, plane, slice(at, at + count), slice(None))]
            for o in (-2, -1, 1, 2):
                other = v[(*slot, child, plane, slice(at + o, at + o + count), slice(None))]
                u = jnp.where(masks[child][o][:count], other, u)
            moved.append(u)
    rows = slice(row, row + count)
    c0, s0 = cos_t[0, tile, rows, :], sin_t[0, tile, rows, :]
    c1, s1 = cos_t[1, tile, rows, :], sin_t[1, tile, rows, :]
    real = (c0 * moved[0] - s0 * moved[1]) + (c1 * moved[2] - s1 * moved[3])
    imag = (s0 * moved[0] + c0 * moved[1]) + (s1 * moved[2] + c1 * moved[3])
    return real, imag


def combine(section, row0, v, slot, masks, cos_t, sin_t, tile, store):
    rows = ROWS[section]
    for row in range(0, rows, 16):
        count = min(16, rows - row)
        parts = merged_rows(v, slot, masks, cos_t, sin_t, tile, row, count)
        if section < 3 and row != 16:
            bins = lax.broadcasted_iota(jnp.int32, (count, LANES), 0) + (row0 + row + BASE[section])
            inside = (bins >= 0) & (bins < STRIPS * STRIP)
            parts = [jnp.where(inside, part, 0.0) for part in parts]
        if count < 16:
            rest = jnp.zeros((16 - count, LANES), F32)
            parts = [jnp.concatenate([part, rest], axis=0) for part in parts]
        for plane in range(2):
            store(plane, row, parts[plane].astype(BF16))


def section_zero(image, row0, recv, shf, band, cos_t, sin_t, v, out):
    for child in range(2):
        lhs = recv[image, :, child].reshape(2 * BLOCK, BEAMS)
        rhs = jnp.concatenate([band[child, t] for t in range(4)], axis=1)
        product = jnp.dot(lhs, rhs, preferred_element_type=F32)
        for plane in range(2):
            for t in range(4):
                v[0, t, child, plane, 0:BLOCK, :] = product[
                    plane * BLOCK : (plane + 1) * BLOCK, t * LANES : (t + 1) * LANES
                ]
    for t in range(4):

        def store(plane, row, value, t=t):
            out[plane, image, row : row + 16, (t + 1) * LANES : (t + 2) * LANES] = value
            if t == 3:
                out[plane, image, row : row + 16, 0:LANES] = value

        combine(0, row0, v, (0, t), masks_of(shf, t), cos_t, sin_t, t, store)


def section_later(section, row0, source, shf, band, cos_t, sin_t, v, out):
    images = 8 >> section
    tiles = TILES[section]

    def tiles_of(block):
        return (lax.rem(2 * block + tiles - 1, tiles), 2 * block)

    def multiply(slot, block):
        window = pl.ds(pl.multiple_of(block * LANES, LANES), BEAMS)
        here = tiles_of(block)
        for child in range(2):
            lhs = source[:, child * images : (child + 1) * images, :, window]
            lhs = lhs.reshape(2 * images * BLOCK, BEAMS)
            rhs = jnp.concatenate([band[child, FIRST[section] + t] for t in here], axis=1)
            product = jnp.dot(lhs, rhs, preferred_element_type=F32)
            for plane in range(2):
                for image in range(images):
                    at = (plane * images + image) * BLOCK
                    for side in range(2):
                        v[slot, 2 * image + side, child, plane, 0:BLOCK, :] = product[
                            at : at + BLOCK, side * LANES : (side + 1) * LANES
                        ]

    def finish(slot, block):
        for side, t in enumerate(tiles_of(block)):
            tile = FIRST[section] + t
            masks = masks_of(shf, tile)
            for image in range(images):

                def store(plane, row, value, side=side, t=t, image=image):
                    if section == 3:
                        cols = pl.ds(pl.multiple_of(t * LANES, LANES), LANES)
                        out[plane, row : row + 16, cols] = value
                        return
                    cols = pl.ds(pl.multiple_of((t + 1) * LANES, LANES), LANES)
                    out[plane, image, row : row + 16, cols] = value
                    if side == 0 and isinstance(block, int) and block == 0:
                        out[plane, image, row : row + 16, 0:LANES] = value

                combine(section, row0, v, (slot, 2 * image + side), masks, cos_t, sin_t, tile, store)

    def step(first):
        multiply(0, first)
        for slot in range(1, SLOTS):
            multiply(slot, first + slot)
            finish(slot - 1, first + slot - 1)
        finish(SLOTS - 1, first + SLOTS - 1)

    def body(turn, carry):
        step(turn * SLOTS)
        return carry

    lax.fori_loop(0, tiles // 2 // SLOTS, body, 0)
    if section < 3:
        out[:, :, :, 0:LANES] = out[:, :, :, tiles * LANES : (tiles + 1) * LANES]


def kernel(
    images, idx_h, shf_h, wts_h, base_h, slope_h, final,
    recv, relay, idx, shf, wts, base, slope, band, cos_t, sin_t, s1, s2, s3, v,
    local_sem, table_sem, send_sem, recv_sem, relay_sem, forward_sem, margin_sem, comm=True, place=None,
):
    if comm:
        sub, q = lax.axis_index("sub"), lax.axis_index("rng")
        z, lane = sub // COLUMN, sub % COLUMN
    else:
        z, q = jnp.int32(place[0]), jnp.int32(place[1])

    def device(zz, qq):
        return (zz * COLUMN + lane, qq)

    groups = TILE // GROUP
    has_next = (z < CHIPS - 1) | (q < STRIPS - 1)
    has_previous = (z > 0) | (q > 0)

    def beside(side):
        if side == 0:
            return device((z + 1) % CHIPS, q + (z == CHIPS - 1).astype(jnp.int32))
        return device((z + CHIPS - 1) % CHIPS, q - (z == 0).astype(jnp.int32))

    if comm:
        barrier = pltpu.get_barrier_semaphore()
        for step in range(1, CHIPS):
            pl.semaphore_signal(
                barrier, inc=1, device_id=device((z + step) % CHIPS, q), device_id_type=MESH
            )
        leaves_up = (z == CHIPS - 1) & (q < STRIPS - 1)
        leaves_down = (z == 0) & (q > 0)
        for side, leaves in enumerate((leaves_up, leaves_down)):

            @pl.when(leaves)
            def _(side=side):
                pl.semaphore_signal(barrier, inc=1, device_id=beside(side), device_id_type=MESH)

    fetches = [
        pltpu.make_async_copy(src, dst, table_sem.at[i])
        for i, (src, dst) in enumerate(
            ((idx_h, idx), (shf_h, shf), (wts_h, wts), (base_h, base), (slope_h, slope))
        )
    ]
    for fetch in fetches:
        fetch.start()

    main = pl.ds(1, groups)

    def of_tile(to, first=0, count=groups):
        return pl.ds(to * groups + first, count)

    if comm:
        own = pltpu.make_async_copy(
            images.at[:, :, of_tile(z)], recv.at[z, :, :, main], local_sem
        )
        own.start()
        peers = CHIPS - 1 + leaves_up.astype(jnp.int32) + leaves_down.astype(jnp.int32)
        pl.semaphore_wait(barrier, peers)

        def block_copy(step):
            to = (z + step) % CHIPS
            return pltpu.make_async_remote_copy(
                src_ref=images.at[:, :, of_tile(to)],
                dst_ref=recv.at[z, :, :, main],
                send_sem=send_sem.at[step],
                recv_sem=recv_sem.at[step],
                device_id=device(to, q),
                device_id_type=MESH,
            )

        def relay_copy(way):
            return pltpu.make_async_remote_copy(
                src_ref=images.at[:, :, of_tile((z + 4) % CHIPS, 2 * way, 2)],
                dst_ref=relay.at[way],
                send_sem=relay_sem.at[0, way],
                recv_sem=relay_sem.at[1, way],
                device_id=device((z + (2, 6)[way]) % CHIPS, q),
                device_id_type=MESH,
            )

        def forward_copy(way):
            return pltpu.make_async_remote_copy(
                src_ref=relay.at[way],
                dst_ref=recv.at[(z + (6, 2)[way]) % CHIPS, :, :, pl.ds(1 + 2 * way, 2)],
                send_sem=forward_sem.at[0, way],
                recv_sem=forward_sem.at[1, way],
                device_id=device((z + (2, 6)[way]) % CHIPS, q),
                device_id_type=MESH,
            )

        def margin_copy(side, image):
            return pltpu.make_async_remote_copy(
                src_ref=recv.at[image, :, :, (groups, 1)[side]],
                dst_ref=recv.at[image, :, :, (0, groups + 1)[side]],
                send_sem=margin_sem.at[0, side, image],
                recv_sem=margin_sem.at[1, side, image],
                device_id=beside(side),
                device_id_type=MESH,
            )

        for way in range(2):
            relay_copy(way).start()
        for step in STEPS:
            block_copy(step).start()

        @pl.when(jnp.logical_not(has_previous))
        def _():
            recv[:, :, :, 0] = jnp.zeros((CHIPS, 2, 2, GROUP, BEAMS), BF16)

        @pl.when(jnp.logical_not(has_next))
        def _():
            recv[:, :, :, groups + 1] = jnp.zeros((CHIPS, 2, 2, GROUP, BEAMS), BF16)
    else:
        own = pltpu.make_async_copy(images, recv, local_sem)
        own.start()

    for fetch in fetches:
        fetch.wait()
    tables = (z, q, idx, shf, wts, base, slope, band, cos_t, sin_t)
    build_tables(*tables, sections=(0, 1, 2))
    if comm:
        for way in range(2):
            relay_copy(way).wait_recv()
            forward_copy(way).start()
    build_tables(*tables, sections=(3,))
    own.wait()
    row0 = q * STRIP + z * TILE

    if comm:

        def spread(image):
            for side, there in enumerate((has_next, has_previous)):

                @pl.when(there)
                def _(side=side):
                    margin_copy(side, image).start()

        spread(z)
        for step in STEPS:
            block_copy(step).wait_recv()
            spread((z + CHIPS - step) % CHIPS)
        for way in range(2):
            forward_copy(way).wait_recv()
        spread((z + 4) % CHIPS)

    def arrival(turn, carry):
        image = (z + turn) % CHIPS
        if comm:
            @pl.when(has_previous)
            def _():
                margin_copy(0, image).wait_recv()

            @pl.when(has_next)
            def _():
                margin_copy(1, image).wait_recv()

        section_zero(image, row0, recv, shf, band, cos_t, sin_t, v, s1)
        return carry

    lax.fori_loop(0, CHIPS, arrival, 0)
    section_later(1, row0, s1, shf, band, cos_t, sin_t, v, s2)
    section_later(2, row0, s2, shf, band, cos_t, sin_t, v, s3)
    section_later(3, row0, s3, shf, band, cos_t, sin_t, v, final)

    if comm:
        for way in range(2):
            relay_copy(way).wait_send()
            forward_copy(way).wait_send()
        for step in STEPS:
            block_copy(step).wait_send()
        for side, there in enumerate((has_next, has_previous)):

            @pl.when(there)
            def _(side=side):
                for image in range(CHIPS):
                    margin_copy(side, image).wait_send()


def call(images, tables, comm=True, place=None):
    vmem = pl.BlockSpec(memory_space=pltpu.VMEM)
    hbm = pl.BlockSpec(memory_space=pltpu.HBM)
    dma = pltpu.SemaphoreType.DMA
    tiles = sum(TILES)
    params = dict(vmem_limit_bytes=62 * 2**20, has_side_effects=True)
    if comm:
        params["collective_id"] = 0
    return pl.pallas_call(
        functools.partial(kernel, comm=comm, place=place),
        out_shape=jax.ShapeDtypeStruct((2, TILE, 4096), BF16),
        in_specs=[hbm] * 6,
        out_specs=vmem,
        scratch_shapes=[
            pltpu.VMEM((CHIPS, 2, 2, BLOCK // GROUP, GROUP, BEAMS), BF16),
            pltpu.VMEM((2, 2, 2, 2, GROUP, BEAMS), BF16),
            *[pltpu.VMEM(table.shape, table.dtype) for table in tables],
            pltpu.VMEM((2, tiles, BEAMS, LANES), BF16),
            pltpu.VMEM((2, tiles, BLOCK, LANES), F32),
            pltpu.VMEM((2, tiles, BLOCK, LANES), F32),
            pltpu.VMEM((2, 8, BLOCK, 512 + LANES), BF16),
            pltpu.VMEM((2, 4, BLOCK, 1024 + LANES), BF16),
            pltpu.VMEM((2, 2, BLOCK, 2048 + LANES), BF16),
            pltpu.VMEM((SLOTS, 8, 2, 2, BLOCK + GROUP, LANES), F32),
            dma,
            dma((len(tables),)),
            dma((CHIPS,)),
            dma((CHIPS,)),
            dma((2, 2)),
            dma((2, 2)),
            dma((2, 2, CHIPS)),
        ],
        compiler_params=pltpu.CompilerParams(**params),
    )(images, *tables)


def local(images, *tables):
    grouped = images.reshape(2, 2, STRIP // GROUP, GROUP, BEAMS)
    return call(grouped, tables).reshape(2, 1, 1, TILE, 4096)


def solution(mesh):
    in_specs = (P(None, "sub", "rng", None), P(), P(), P(), P(), P())
    out_specs = P(None, "sub", "rng", None, None)
    return jax.shard_map(local, mesh=mesh, in_specs=in_specs, out_specs=out_specs, check_vma=False)
```

```python
import functools

import jax
import jax.numpy as jnp
from jax import lax
from jax.experimental import pallas as pl
from jax.experimental.pallas import tpu as pltpu
from jax.sharding import PartitionSpec as P

MESH = pl.DeviceIdType.MESH
BF16 = jnp.bfloat16
F32 = jnp.float32
CHIPS = 8
COLUMN = 8
STRIPS = 4
STRIP = 256
TILE = 32
HALO = 8
BLOCK = TILE + 2 * HALO
GROUP = 8
BEAMS = 256
LANES = 128
TAPS = 4
SHIFT = 2
TILES = (4, 8, 16, 32)
FIRST = (0, 4, 12, 28)
ROWS = (48, 40, 40, 32)
BASE = (-6, -4, -2, 0)
BAND_ROWS = 96
STEPS = (3, 5, 2, 6, 1, 7)
SLOTS = 4


def build_tables(z, q, idx, shf, wts, base, slope, band, cos_t, sin_t, sections):
    origin_row = q * STRIP + z * TILE
    iota8 = lax.broadcasted_iota(jnp.int32, (8, LANES), 0)
    iota_k = lax.broadcasted_iota(jnp.int32, (BAND_ROWS, LANES), 0)

    def one(section, child, tile, origin, offset):
        cols = pl.ds(pl.multiple_of(tile * LANES, LANES), LANES)
        band[child, tile] = jnp.zeros((BEAMS, LANES), BF16)
        first = idx[child : child + 1, cols] - (origin + offset)
        weights = wts[child, :, cols].astype(F32)
        patch = jnp.zeros((BAND_ROWS, LANES), F32)
        for tap in range(TAPS):
            patch = jnp.where(iota_k == first + tap, weights[tap : tap + 1, :], patch)
        if not isinstance(offset, int):
            offset = pl.multiple_of(offset, 16)
        band[child, tile, pl.ds(offset, BAND_ROWS), :] = patch.astype(BF16)
        rate = slope[child : child + 1, cols]
        rows = (iota8 + (origin_row + BASE[section])).astype(F32)
        theta = base[child : child + 1, cols] + rate * rows
        c, s = jnp.cos(theta), jnp.sin(theta)
        turn = jnp.broadcast_to(rate * 8.0, (8, LANES))
        c8, s8 = jnp.cos(turn), jnp.sin(turn)
        for step in range(ROWS[section] // 8):
            cos_t[child, tile, step * 8 : step * 8 + 8, :] = c
            sin_t[child, tile, step * 8 : step * 8 + 8, :] = s
            c, s = c * c8 - s * s8, s * c8 + c * s8

    for child in range(2 if 0 in sections else 0):
        for tile in range(TILES[0]):
            one(0, child, tile, 0, (0, 48, 112, 160)[tile])
    for section in sections:
        if section == 0:
            continue
        tiles = TILES[section]

        def body(tile, carry, section=section, tiles=tiles):
            block = (tile + 1) // 2
            side = (tile + 1) % 2
            for child in range(2):
                one(section, child, FIRST[section] + tile, LANES * (block - 1), 48 + 64 * side)
            return carry

        lax.fori_loop(0, tiles, body, 0)


def masks_of(shf, tile):
    found = []
    for child in range(2):
        cols = pl.ds(pl.multiple_of(tile * LANES, LANES), LANES)
        row = jnp.broadcast_to(shf[child : child + 1, cols], (16, LANES))
        found.append({o: row == o for o in (-2, -1, 1, 2)})
    return found


def pieces_of(section, part):
    if part == 1:
        low, high = (0, 24) if section == 3 else (32, 56)
        return (
            (2, 0, 8, ((low, 0, 8, 8),)),
            (22, 36 - 4 * section, 8, ((high, 0, 8, 8),)),
        )
    if section == 3:
        return ((2, 8, 16, ((8, 0, 8, 8), (16, 8, 8, 8))),)
    start = (2, 8, 16, ((0, 0, 16, 16), (40, 0, 8, 8)))
    if section == 0:
        return (start, (18, 24, 16, ((16, 0, 16, 16),)), (22, 28, 8, ((48, 0, 8, 8),)))
    if section == 1:
        return (start, (18, 24, 8, ((16, 0, 8, 16), (48, 0, 8, 8))))
    return (start, (18, 24, 8, ((16, 0, 8, 16),)), (14, 20, 8, ((48, 0, 8, 8),)))


def combine(section, part, row0, v, slot, masks, cos_t, sin_t, tile, store):
    for at, phase, count, places in pieces_of(section, part):
        moved = []
        for child in range(2):
            for plane in range(2):
                u = v[(*slot, child, plane, slice(at, at + count), slice(None))]
                for o in (-2, -1, 1, 2):
                    other = v[(*slot, child, plane, slice(at + o, at + o + count), slice(None))]
                    u = jnp.where(masks[child][o][:count], other, u)
                moved.append(u)
        rows = slice(phase, phase + count)
        c0, s0 = cos_t[0, tile, rows, :], sin_t[0, tile, rows, :]
        c1, s1 = cos_t[1, tile, rows, :], sin_t[1, tile, rows, :]
        parts = [
            (c0 * moved[0] - s0 * moved[1]) + (c1 * moved[2] - s1 * moved[3]),
            (s0 * moved[0] + c0 * moved[1]) + (s1 * moved[2] + c1 * moved[3]),
        ]
        if part == 1 and section < 3:
            bins = lax.broadcasted_iota(jnp.int32, (count, LANES), 0)
            bins = bins + (row0 + phase + BASE[section])
            inside = (bins >= 0) & (bins < STRIPS * STRIP)
            parts = [jnp.where(inside, value, 0.0) for value in parts]
        for to, first, taken, written in places:
            for plane in range(2):
                value = parts[plane][first : first + taken]
                if written > taken:
                    rest = jnp.zeros((written - taken, LANES), F32)
                    value = jnp.concatenate([value, rest], axis=0)
                store(plane, slice(to, to + written), value.astype(BF16))


def section_zero(images, part, row0, recv, shf, band, cos_t, sin_t, v, out):
    def slot_of(k, t):
        return (k // 2, (k % 2) * 4 + t)

    for k, image in enumerate(images):
        for child in range(2):
            if part == 0:
                lhs = recv[image, :, child, 1:5].reshape(2 * 32, BEAMS)
            else:
                ends = [recv[image, :, child, at : at + 2].reshape(2, 16, BEAMS) for at in (0, 4)]
                lhs = jnp.concatenate(ends, axis=1).reshape(2 * 32, BEAMS)
            rhs = jnp.concatenate([band[child, t] for t in range(4)], axis=1)
            product = jnp.dot(lhs, rhs, preferred_element_type=F32)
            for plane in range(2):
                for t in range(4):
                    v[(*slot_of(k, t), child, plane, slice(0, 32), slice(None))] = product[
                        plane * 32 : (plane + 1) * 32, t * LANES : (t + 1) * LANES
                    ]
    for t in range(4):
        masks = masks_of(shf, t)
        for k, image in enumerate(images):

            def store(plane, rows, value, t=t, image=image):
                out[plane, image, rows, (t + 1) * LANES : (t + 2) * LANES] = value
                if t == 3:
                    out[plane, image, rows, 0:LANES] = value

            combine(0, part, row0, v, slot_of(k, t), masks, cos_t, sin_t, t, store)


def section_later(section, part, row0, source, shf, band, cos_t, sin_t, v, out):
    images = 8 >> section
    tiles = TILES[section]
    half = slice(part * 32, part * 32 + 32)

    def tiles_of(block):
        return (lax.rem(2 * block + tiles - 1, tiles), 2 * block)

    def multiply(slot, block):
        window = pl.ds(pl.multiple_of(block * LANES, LANES), BEAMS)
        here = tiles_of(block)
        for child in range(2):
            lhs = source[:, child * images : (child + 1) * images, half, window]
            lhs = lhs.reshape(2 * images * 32, BEAMS)
            rhs = jnp.concatenate([band[child, FIRST[section] + t] for t in here], axis=1)
            product = jnp.dot(lhs, rhs, preferred_element_type=F32)
            for plane in range(2):
                for image in range(images):
                    at = (plane * images + image) * 32
                    for side in range(2):
                        v[slot, 2 * image + side, child, plane, 0:32, :] = product[
                            at : at + 32, side * LANES : (side + 1) * LANES
                        ]

    def finish(slot, block):
        for side, t in enumerate(tiles_of(block)):
            tile = FIRST[section] + t
            masks = masks_of(shf, tile)
            for image in range(images):

                def store(plane, rows, value, t=t, image=image):
                    if section == 3:
                        cols = pl.ds(pl.multiple_of(t * LANES, LANES), LANES)
                        out[plane, rows, cols] = value
                    else:
                        cols = pl.ds(pl.multiple_of((t + 1) * LANES, LANES), LANES)
                        out[plane, image, rows, cols] = value

                slots = (slot, 2 * image + side)
                combine(section, part, row0, v, slots, masks, cos_t, sin_t, tile, store)

    def body(turn, carry):
        first = turn * SLOTS
        multiply(0, first)
        for slot in range(1, SLOTS):
            multiply(slot, first + slot)
            finish(slot - 1, first + slot - 1)
        finish(SLOTS - 1, first + SLOTS - 1)
        return carry

    lax.fori_loop(0, tiles // 2 // SLOTS, body, 0)
    if section < 3:
        out[:, :, half, 0:LANES] = out[:, :, half, tiles * LANES : (tiles + 1) * LANES]


def kernel(
    images, idx_h, shf_h, wts_h, base_h, slope_h, final,
    recv, relay, idx, shf, wts, base, slope, band, cos_t, sin_t, s1, s2, s3, v,
    local_sem, table_sem, send_sem, recv_sem, relay_sem, forward_sem, margin_sem, comm=True, place=None,
):
    if comm:
        sub, q = lax.axis_index("sub"), lax.axis_index("rng")
        z, lane = sub // COLUMN, sub % COLUMN
    else:
        z, q = jnp.int32(place[0]), jnp.int32(place[1])

    def device(zz, qq):
        return (zz * COLUMN + lane, qq)

    groups = TILE // GROUP
    has_next = (z < CHIPS - 1) | (q < STRIPS - 1)
    has_previous = (z > 0) | (q > 0)

    def beside(side):
        if side == 0:
            return device((z + 1) % CHIPS, q + (z == CHIPS - 1).astype(jnp.int32))
        return device((z + CHIPS - 1) % CHIPS, q - (z == 0).astype(jnp.int32))

    if comm:
        barrier = pltpu.get_barrier_semaphore()
        for step in range(1, CHIPS):
            pl.semaphore_signal(
                barrier, inc=1, device_id=device((z + step) % CHIPS, q), device_id_type=MESH
            )
        leaves_up = (z == CHIPS - 1) & (q < STRIPS - 1)
        leaves_down = (z == 0) & (q > 0)
        for side, leaves in enumerate((leaves_up, leaves_down)):

            @pl.when(leaves)
            def _(side=side):
                pl.semaphore_signal(barrier, inc=1, device_id=beside(side), device_id_type=MESH)

    fetches = [
        pltpu.make_async_copy(src, dst, table_sem.at[i])
        for i, (src, dst) in enumerate(
            ((idx_h, idx), (shf_h, shf), (wts_h, wts), (base_h, base), (slope_h, slope))
        )
    ]
    for fetch in fetches:
        fetch.start()

    main = pl.ds(1, groups)

    def of_tile(to, first=0, count=groups):
        return pl.ds(to * groups + first, count)

    if comm:
        own = pltpu.make_async_copy(
            images.at[:, :, of_tile(z)], recv.at[z, :, :, main], local_sem
        )
        own.start()
        peers = CHIPS - 1 + leaves_up.astype(jnp.int32) + leaves_down.astype(jnp.int32)
        pl.semaphore_wait(barrier, peers)

        def block_copy(step):
            to = (z + step) % CHIPS
            return pltpu.make_async_remote_copy(
                src_ref=images.at[:, :, of_tile(to)],
                dst_ref=recv.at[z, :, :, main],
                send_sem=send_sem.at[step],
                recv_sem=recv_sem.at[step],
                device_id=device(to, q),
                device_id_type=MESH,
            )

        def relay_copy(way):
            return pltpu.make_async_remote_copy(
                src_ref=images.at[:, :, of_tile((z + 4) % CHIPS, 2 * way, 2)],
                dst_ref=relay.at[way],
                send_sem=relay_sem.at[0, way],
                recv_sem=relay_sem.at[1, way],
                device_id=device((z + (2, 6)[way]) % CHIPS, q),
                device_id_type=MESH,
            )

        def forward_copy(way):
            return pltpu.make_async_remote_copy(
                src_ref=relay.at[way],
                dst_ref=recv.at[(z + (6, 2)[way]) % CHIPS, :, :, pl.ds(1 + 2 * way, 2)],
                send_sem=forward_sem.at[0, way],
                recv_sem=forward_sem.at[1, way],
                device_id=device((z + (2, 6)[way]) % CHIPS, q),
                device_id_type=MESH,
            )

        def margin_copy(side, image):
            return pltpu.make_async_remote_copy(
                src_ref=recv.at[image, :, :, (groups, 1)[side]],
                dst_ref=recv.at[image, :, :, (0, groups + 1)[side]],
                send_sem=margin_sem.at[0, side, image],
                recv_sem=margin_sem.at[1, side, image],
                device_id=beside(side),
                device_id_type=MESH,
            )

        for way in range(2):
            relay_copy(way).start()
        for step in STEPS:
            block_copy(step).start()

        @pl.when(jnp.logical_not(has_previous))
        def _():
            recv[:, :, :, 0] = jnp.zeros((CHIPS, 2, 2, GROUP, BEAMS), BF16)

        @pl.when(jnp.logical_not(has_next))
        def _():
            recv[:, :, :, groups + 1] = jnp.zeros((CHIPS, 2, 2, GROUP, BEAMS), BF16)
    else:
        own = pltpu.make_async_copy(images, recv, local_sem)
        own.start()

    for fetch in fetches:
        fetch.wait()
    tables = (z, q, idx, shf, wts, base, slope, band, cos_t, sin_t)
    build_tables(*tables, sections=(0, 1, 2))
    if comm:
        for way in range(2):
            relay_copy(way).wait_recv()
            forward_copy(way).start()
    build_tables(*tables, sections=(3,))
    own.wait()
    row0 = q * STRIP + z * TILE

    def arrival(turn, carry):
        far = 3 - (turn - 1) // 2
        step = jnp.where(turn % 2 == 1, far, CHIPS - far)
        step = jnp.where(turn == 0, 0, jnp.where(turn == CHIPS - 1, 4, step))
        image = (z + CHIPS - step) % CHIPS
        if comm:

            @pl.when((turn > 0) & (turn < CHIPS - 1))
            def _():
                block_copy(step).wait_recv()

            @pl.when(turn == CHIPS - 1)
            def _():
                for way in range(2):
                    forward_copy(way).wait_recv()

            for side, there in enumerate((has_next, has_previous)):

                @pl.when(there)
                def _(side=side):
                    margin_copy(side, image).start()

        section_zero([image], 0, row0, recv, shf, band, cos_t, sin_t, v, s1)
        return carry

    def margins(image, carry):
        if comm:

            @pl.when(has_previous)
            def _():
                margin_copy(0, image).wait_recv()

            @pl.when(has_next)
            def _():
                margin_copy(1, image).wait_recv()

        return carry

    def outer(turn, carry):
        images = [turn * 4 + k for k in range(4)]
        section_zero(images, 1, row0, recv, shf, band, cos_t, sin_t, v, s1)
        return carry

    arrays = (s1, s2, s3, final)
    for part in range(2):
        if part == 0:
            lax.fori_loop(0, CHIPS, arrival, 0)
        else:
            lax.fori_loop(0, CHIPS, margins, 0)
            lax.fori_loop(0, CHIPS // 4, outer, 0)
        for section in range(1, 4):
            source, out = arrays[section - 1 : section + 1]
            section_later(section, part, row0, source, shf, band, cos_t, sin_t, v, out)

    if comm:
        for way in range(2):
            relay_copy(way).wait_send()
            forward_copy(way).wait_send()
        for step in STEPS:
            block_copy(step).wait_send()
        for side, there in enumerate((has_next, has_previous)):

            @pl.when(there)
            def _(side=side):
                for image in range(CHIPS):
                    margin_copy(side, image).wait_send()


def call(images, tables, comm=True, place=None):
    vmem = pl.BlockSpec(memory_space=pltpu.VMEM)
    hbm = pl.BlockSpec(memory_space=pltpu.HBM)
    dma = pltpu.SemaphoreType.DMA
    tiles = sum(TILES)
    params = dict(vmem_limit_bytes=48 * 2**20, has_side_effects=True)
    if comm:
        params["collective_id"] = 0
    return pl.pallas_call(
        functools.partial(kernel, comm=comm, place=place),
        out_shape=jax.ShapeDtypeStruct((2, TILE, 4096), BF16),
        in_specs=[hbm] * 6,
        out_specs=vmem,
        scratch_shapes=[
            pltpu.VMEM((CHIPS, 2, 2, BLOCK // GROUP, GROUP, BEAMS), BF16),
            pltpu.VMEM((2, 2, 2, 2, GROUP, BEAMS), BF16),
            *[pltpu.VMEM(table.shape, table.dtype) for table in tables],
            pltpu.VMEM((2, tiles, BEAMS, LANES), BF16),
            pltpu.VMEM((2, tiles, BLOCK, LANES), F32),
            pltpu.VMEM((2, tiles, BLOCK, LANES), F32),
            pltpu.VMEM((2, 8, 64, 512 + LANES), BF16),
            pltpu.VMEM((2, 4, 64, 1024 + LANES), BF16),
            pltpu.VMEM((2, 2, 64, 2048 + LANES), BF16),
            pltpu.VMEM((SLOTS, 8, 2, 2, 40, LANES), F32),
            dma,
            dma((len(tables),)),
            dma((CHIPS,)),
            dma((CHIPS,)),
            dma((2, 2)),
            dma((2, 2)),
            dma((2, 2, CHIPS)),
        ],
        compiler_params=pltpu.CompilerParams(**params),
    )(images, *tables)


def local(images, *tables):
    grouped = images.reshape(2, 2, STRIP // GROUP, GROUP, BEAMS)
    grouped, *tables = (pltpu.with_memory_space_constraint(x, pltpu.HBM) for x in (grouped, *tables))
    return call(grouped, tables).reshape(2, 1, 1, TILE, 4096)


def solution(mesh):
    in_specs = (P(None, "sub", "rng", None), P(), P(), P(), P(), P())
    out_specs = P(None, "sub", "rng", None, None)
    return jax.shard_map(local, mesh=mesh, in_specs=in_specs, out_specs=out_specs, check_vma=False)
```

```python
import functools

import jax
import jax.numpy as jnp
from jax import lax
from jax.experimental import pallas as pl
from jax.experimental.pallas import tpu as pltpu
from jax.sharding import PartitionSpec as P

MESH = pl.DeviceIdType.MESH
BF16 = jnp.bfloat16
F32 = jnp.float32
CHIPS = 8
COLUMN = 8
STRIPS = 4
STRIP = 256
TILE = 32
HALO = 8
BLOCK = TILE + 2 * HALO
GROUP = 8
BEAMS = 256
LANES = 128
TAPS = 4
SHIFT = 2
TILES = (4, 8, 16, 32)
FIRST = (0, 4, 12, 28)
ROWS = (48, 40, 40, 32)
BASE = (-6, -4, -2, 0)
BAND_ROWS = 96
MARGINS = ((4, 1, 7, 2), (0, 6, 3, 5))
STEPS = (3, 5, 2, 6, 1, 7)


def build_tables(z, q, idx, shf, wts, base, slope, band, cos_t, sin_t, sections):
    origin_row = q * STRIP + z * TILE
    iota8 = lax.broadcasted_iota(jnp.int32, (8, LANES), 0)
    iota_k = lax.broadcasted_iota(jnp.int32, (BAND_ROWS, LANES), 0)

    def one(section, child, tile, origin, offset):
        cols = pl.ds(pl.multiple_of(tile * LANES, LANES), LANES)
        band[child, tile] = jnp.zeros((BEAMS, LANES), BF16)
        first = idx[child : child + 1, cols] - (origin + offset)
        weights = wts[child, :, cols].astype(F32)
        patch = jnp.zeros((BAND_ROWS, LANES), F32)
        for tap in range(TAPS):
            patch = jnp.where(iota_k == first + tap, weights[tap : tap + 1, :], patch)
        if not isinstance(offset, int):
            offset = pl.multiple_of(offset, 16)
        band[child, tile, pl.ds(offset, BAND_ROWS), :] = patch.astype(BF16)
        rate = slope[child : child + 1, cols]
        rows = (iota8 + (origin_row + BASE[section])).astype(F32)
        theta = base[child : child + 1, cols] + rate * rows
        c, s = jnp.cos(theta), jnp.sin(theta)
        turn = jnp.broadcast_to(rate * 8.0, (8, LANES))
        c8, s8 = jnp.cos(turn), jnp.sin(turn)
        for step in range(ROWS[section] // 8):
            cos_t[child, tile, step * 8 : step * 8 + 8, :] = c
            sin_t[child, tile, step * 8 : step * 8 + 8, :] = s
            c, s = c * c8 - s * s8, s * c8 + c * s8

    for child in range(2 if 0 in sections else 0):
        for tile in range(TILES[0]):
            one(0, child, tile, 0, (0, 48, 112, 160)[tile])
    for section in sections:
        if section == 0:
            continue
        tiles = TILES[section]

        def body(tile, carry, section=section, tiles=tiles):
            block = (tile + 1) // 2
            side = (tile + 1) % 2
            for child in range(2):
                one(section, child, FIRST[section] + tile, LANES * (block - 1), 48 + 64 * side)
            return carry

        lax.fori_loop(0, tiles, body, 0)


def masks_of(shf, tile):
    found = []
    for child in range(2):
        cols = pl.ds(pl.multiple_of(tile * LANES, LANES), LANES)
        row = jnp.broadcast_to(shf[child : child + 1, cols], (16, LANES))
        found.append({o: row == o for o in (-2, -1, 1, 2)})
    return found


def pieces_of(section, part):
    if part == 1:
        low, high = (0, 24) if section == 3 else (32, 56)
        return (
            (2, 0, 8, ((low, 0, 8, 8),)),
            (22, 36 - 4 * section, 8, ((high, 0, 8, 8),)),
        )
    if section == 3:
        return ((2, 8, 16, ((8, 0, 8, 8), (16, 8, 8, 8))),)
    start = (2, 8, 16, ((0, 0, 16, 16), (40, 0, 8, 8)))
    if section == 0:
        return (start, (18, 24, 16, ((16, 0, 16, 16),)), (22, 28, 8, ((48, 0, 8, 8),)))
    if section == 1:
        return (start, (18, 24, 8, ((16, 0, 8, 16), (48, 0, 8, 8))))
    return (start, (18, 24, 8, ((16, 0, 8, 16),)), (14, 20, 8, ((48, 0, 8, 8),)))


def combine(section, part, row0, v, slot, masks, cos_t, sin_t, tile, store):
    for at, phase, count, places in pieces_of(section, part):
        moved = []
        for child in range(2):
            for plane in range(2):
                u = v[(*slot, child, plane, slice(at, at + count), slice(None))]
                for o in (-2, -1, 1, 2):
                    other = v[(*slot, child, plane, slice(at + o, at + o + count), slice(None))]
                    u = jnp.where(masks[child][o][:count], other, u)
                moved.append(u)
        rows = slice(phase, phase + count)
        c0, s0 = cos_t[0, tile, rows, :], sin_t[0, tile, rows, :]
        c1, s1 = cos_t[1, tile, rows, :], sin_t[1, tile, rows, :]
        parts = [
            (c0 * moved[0] - s0 * moved[1]) + (c1 * moved[2] - s1 * moved[3]),
            (s0 * moved[0] + c0 * moved[1]) + (s1 * moved[2] + c1 * moved[3]),
        ]
        if part == 1 and section < 3:
            bins = lax.broadcasted_iota(jnp.int32, (count, LANES), 0)
            bins = bins + (row0 + phase + BASE[section])
            inside = (bins >= 0) & (bins < STRIPS * STRIP)
            parts = [jnp.where(inside, value, 0.0) for value in parts]
        for to, first, taken, written in places:
            for plane in range(2):
                value = parts[plane][first : first + taken]
                if written > taken:
                    rest = jnp.zeros((written - taken, LANES), F32)
                    value = jnp.concatenate([value, rest], axis=0)
                store(plane, slice(to, to + written), value.astype(BF16))


def section_zero(images, part, row0, recv, shf, band, cos_t, sin_t, v, out):
    def slot_of(k, t):
        return (k // 2, (k % 2) * 4 + t)

    for k, image in enumerate(images):
        for child in range(2):
            if part == 0:
                lhs = recv[image, :, child, 1:5].reshape(2 * 32, BEAMS)
            else:
                ends = [recv[image, :, child, at : at + 2].reshape(2, 16, BEAMS) for at in (0, 4)]
                lhs = jnp.concatenate(ends, axis=1).reshape(2 * 32, BEAMS)
            rhs = jnp.concatenate([band[child, t] for t in range(4)], axis=1)
            product = jnp.dot(lhs, rhs, preferred_element_type=F32)
            for plane in range(2):
                for t in range(4):
                    v[(*slot_of(k, t), child, plane, slice(0, 32), slice(None))] = product[
                        plane * 32 : (plane + 1) * 32, t * LANES : (t + 1) * LANES
                    ]
    for t in range(4):
        masks = masks_of(shf, t)
        for k, image in enumerate(images):

            def store(plane, rows, value, t=t, image=image):
                out[plane, image, rows, t * LANES : (t + 1) * LANES] = value

            combine(0, part, row0, v, slot_of(k, t), masks, cos_t, sin_t, t, store)


def section_later(section, part, row0, source, shf, band, cos_t, sin_t, v, out):
    images = 8 >> section
    tiles = TILES[section]
    rows = 32
    half = slice(part * 32, part * 32 + rows)

    blocks = tiles // 2

    def tiles_of(block):
        return ((2 * block - 1) % tiles, 2 * block)

    def slot_of(block, image, side):
        n = (block * images + image) * 2 + side
        return (n // 8, n % 8)

    def multiply(block):
        here = tiles_of(block)
        for child in range(2):
            members = slice(child * images, (child + 1) * images)
            halves = [
                source[:, members, half, t * LANES : (t + 1) * LANES]
                for t in ((block - 1) % blocks, block)
            ]
            lhs = jnp.concatenate(halves, axis=3)
            lhs = lhs.reshape(2 * images * rows, BEAMS)
            rhs = jnp.concatenate([band[child, FIRST[section] + t] for t in here], axis=1)
            product = jnp.dot(lhs, rhs, preferred_element_type=F32)
            for plane in range(2):
                for image in range(images):
                    at = (plane * images + image) * rows
                    for side in range(2):
                        to = (*slot_of(block, image, side), child, plane, slice(0, rows), slice(None))
                        v[to] = product[at : at + rows, side * LANES : (side + 1) * LANES]

    def finish(block):
        for side, t in enumerate(tiles_of(block)):
            tile = FIRST[section] + t
            masks = masks_of(shf, tile)
            cols = slice(t * LANES, (t + 1) * LANES)
            for image in range(images):

                def store(plane, rows, value, cols=cols, image=image):
                    if section == 3:
                        out[plane, rows, cols] = value
                    else:
                        out[plane, image, rows, cols] = value

                slots = slot_of(block, image, side)
                combine(section, part, row0, v, slots, masks, cos_t, sin_t, tile, store)

    order = [*range(1, blocks), 0]
    multiply(order[0])
    for now, later in zip(order, order[1:]):
        multiply(later)
        finish(now)
    finish(order[-1])


def kernel(
    images, idx_h, shf_h, wts_h, base_h, slope_h, final,
    recv, relay, idx, shf, wts, base, slope, band, cos_t, sin_t, s1, s2, s3, v0, v1, v2, v3,
    local_sem, table_sem, send_sem, recv_sem, relay_sem, forward_sem, margin_sem, comm=True, place=None,
):
    if comm:
        sub, q = lax.axis_index("sub"), lax.axis_index("rng")
        z, lane = sub // COLUMN, sub % COLUMN
    else:
        z, q = jnp.int32(place[0]), jnp.int32(place[1])

    def device(zz, qq):
        return (zz * COLUMN + lane, qq)

    groups = TILE // GROUP
    has_next = (z < CHIPS - 1) | (q < STRIPS - 1)
    has_previous = (z > 0) | (q > 0)

    def beside(side):
        if side == 0:
            return device((z + 1) % CHIPS, q + (z == CHIPS - 1).astype(jnp.int32))
        return device((z + CHIPS - 1) % CHIPS, q - (z == 0).astype(jnp.int32))

    if comm:
        barrier = pltpu.get_barrier_semaphore()
        for step in range(1, CHIPS):
            pl.semaphore_signal(
                barrier, inc=1, device_id=device((z + step) % CHIPS, q), device_id_type=MESH
            )
        leaves_up = (z == CHIPS - 1) & (q < STRIPS - 1)
        leaves_down = (z == 0) & (q > 0)
        for side, leaves in enumerate((leaves_up, leaves_down)):

            @pl.when(leaves)
            def _(side=side):
                pl.semaphore_signal(barrier, inc=1, device_id=beside(side), device_id_type=MESH)

    fetches = [
        pltpu.make_async_copy(src, dst, table_sem.at[i])
        for i, (src, dst) in enumerate(
            ((idx_h, idx), (shf_h, shf), (wts_h, wts), (base_h, base), (slope_h, slope))
        )
    ]
    for fetch in fetches:
        fetch.start()

    main = pl.ds(1, groups)

    def of_tile(to, first=0, count=groups):
        return pl.ds(to * groups + first, count)

    if comm:
        own = pltpu.make_async_copy(
            images.at[:, :, of_tile(z)], recv.at[z, :, :, main], local_sem
        )
        own.start()
        peers = CHIPS - 1 + leaves_up.astype(jnp.int32) + leaves_down.astype(jnp.int32)
        pl.semaphore_wait(barrier, peers)

        def block_copy(step):
            to = (z + step) % CHIPS
            return pltpu.make_async_remote_copy(
                src_ref=images.at[:, :, of_tile(to)],
                dst_ref=recv.at[z, :, :, main],
                send_sem=send_sem.at[step],
                recv_sem=recv_sem.at[step],
                device_id=device(to, q),
                device_id_type=MESH,
            )

        def relay_copy(way):
            return pltpu.make_async_remote_copy(
                src_ref=images.at[:, :, of_tile((z + 4) % CHIPS, 2 * way, 2)],
                dst_ref=relay.at[way],
                send_sem=relay_sem.at[0, way],
                recv_sem=relay_sem.at[1, way],
                device_id=device((z + (2, 6)[way]) % CHIPS, q),
                device_id_type=MESH,
            )

        def forward_copy(way):
            return pltpu.make_async_remote_copy(
                src_ref=relay.at[way],
                dst_ref=recv.at[(z + (6, 2)[way]) % CHIPS, :, :, pl.ds(1 + 2 * way, 2)],
                send_sem=forward_sem.at[0, way],
                recv_sem=forward_sem.at[1, way],
                device_id=device((z + (2, 6)[way]) % CHIPS, q),
                device_id_type=MESH,
            )

        def margin_copy(side, image):
            return pltpu.make_async_remote_copy(
                src_ref=recv.at[image, :, :, (groups, 1)[side]],
                dst_ref=recv.at[image, :, :, (0, groups + 1)[side]],
                send_sem=margin_sem.at[0, side, image],
                recv_sem=margin_sem.at[1, side, image],
                device_id=beside(side),
                device_id_type=MESH,
            )

        for way in range(2):
            relay_copy(way).start()
        for step in STEPS:
            block_copy(step).start()

        @pl.when(jnp.logical_not(has_previous))
        def _():
            recv[:, :, :, 0] = jnp.zeros((CHIPS, 2, 2, GROUP, BEAMS), BF16)

        @pl.when(jnp.logical_not(has_next))
        def _():
            recv[:, :, :, groups + 1] = jnp.zeros((CHIPS, 2, 2, GROUP, BEAMS), BF16)
    else:
        own = pltpu.make_async_copy(images, recv, local_sem)
        own.start()

    for fetch in fetches:
        fetch.wait()
    tables = (z, q, idx, shf, wts, base, slope, band, cos_t, sin_t)
    build_tables(*tables, sections=(0, 1, 2))
    if comm:
        for way in range(2):
            relay_copy(way).wait_recv()
            forward_copy(way).start()
    build_tables(*tables, sections=(3,))
    own.wait()
    row0 = q * STRIP + z * TILE

    def arrival(turn, carry):
        far = 3 - (turn - 1) // 2
        step = jnp.where(turn % 2 == 1, far, CHIPS - far)
        step = jnp.where(turn == 0, 0, jnp.where(turn == CHIPS - 1, 4, step))
        image = (z + CHIPS - step) % CHIPS
        if comm:

            @pl.when((turn > 0) & (turn < CHIPS - 1))
            def _():
                block_copy(step).wait_recv()

            @pl.when(turn == CHIPS - 1)
            def _():
                for way in range(2):
                    forward_copy(way).wait_recv()

            for side, there in enumerate((has_next, has_previous)):

                @pl.when(there)
                def _(side=side):
                    margin_copy(side, image).start()

        section_zero([image], 0, row0, recv, shf, band, cos_t, sin_t, v0, s1)
        return carry

    def outer(images):
        if comm:
            for image in images:

                @pl.when(has_previous)
                def _(image=image):
                    margin_copy(0, image).wait_recv()

                @pl.when(has_next)
                def _(image=image):
                    margin_copy(1, image).wait_recv()

        section_zero(images, 1, row0, recv, shf, band, cos_t, sin_t, v0, s1)

    def later(part):
        for section, source, v, out in ((1, s1, v1, s2), (2, s2, v2, s3), (3, s3, v3, final)):
            section_later(section, part, row0, source, shf, band, cos_t, sin_t, v, out)

    lax.fori_loop(0, CHIPS, arrival, 0)
    later(0)
    for turn in MARGINS:
        outer([(z + CHIPS - step) % CHIPS for step in turn])
    later(1)

    if comm:
        for way in range(2):
            relay_copy(way).wait_send()
            forward_copy(way).wait_send()
        for step in STEPS:
            block_copy(step).wait_send()
        for side, there in enumerate((has_next, has_previous)):

            @pl.when(there)
            def _(side=side):
                for image in range(CHIPS):
                    margin_copy(side, image).wait_send()


def call(images, tables, comm=True, place=None):
    vmem = pl.BlockSpec(memory_space=pltpu.VMEM)
    hbm = pl.BlockSpec(memory_space=pltpu.HBM)
    dma = pltpu.SemaphoreType.DMA
    tiles = sum(TILES)
    params = dict(vmem_limit_bytes=48 * 2**20, has_side_effects=True)
    if comm:
        params["collective_id"] = 0
    return pl.pallas_call(
        functools.partial(kernel, comm=comm, place=place),
        out_shape=jax.ShapeDtypeStruct((2, TILE, 4096), BF16),
        in_specs=[hbm] * 6,
        out_specs=vmem,
        scratch_shapes=[
            pltpu.VMEM((CHIPS, 2, 2, BLOCK // GROUP, GROUP, BEAMS), BF16),
            pltpu.VMEM((2, 2, 2, 2, GROUP, BEAMS), BF16),
            *[pltpu.VMEM(table.shape, table.dtype) for table in tables],
            pltpu.VMEM((2, tiles, BEAMS, LANES), BF16),
            pltpu.VMEM((2, tiles, BLOCK, LANES), F32),
            pltpu.VMEM((2, tiles, BLOCK, LANES), F32),
            pltpu.VMEM((2, 8, 64, 512), BF16),
            pltpu.VMEM((2, 4, 64, 1024), BF16),
            pltpu.VMEM((2, 2, 64, 2048), BF16),
            *[pltpu.VMEM((4, 8, 2, 2, count, LANES), F32) for count in (40, 40, 40, 40)],
            dma,
            dma((len(tables),)),
            dma((CHIPS,)),
            dma((CHIPS,)),
            dma((2, 2)),
            dma((2, 2)),
            dma((2, 2, CHIPS)),
        ],
        compiler_params=pltpu.CompilerParams(**params),
    )(images, *tables)


def local(images, *tables):
    grouped = images.reshape(2, 2, STRIP // GROUP, GROUP, BEAMS)
    grouped, *tables = (pltpu.with_memory_space_constraint(x, pltpu.HBM) for x in (grouped, *tables))
    return call(grouped, tables).reshape(2, 1, 1, TILE, 4096)


def solution(mesh):
    in_specs = (P(None, "sub", "rng", None), P(), P(), P(), P(), P())
    out_specs = P(None, "sub", "rng", None, None)
    return jax.shard_map(local, mesh=mesh, in_specs=in_specs, out_specs=out_specs, check_vma=False)
```

```python
import functools

import jax
import jax.numpy as jnp
from jax import lax
from jax.experimental import pallas as pl
from jax.experimental.pallas import tpu as pltpu
from jax.sharding import PartitionSpec as P

MESH = pl.DeviceIdType.MESH
BF16 = jnp.bfloat16
F32 = jnp.float32
CHIPS = 8
COLUMN = 8
STRIPS = 4
STRIP = 256
TILE = 32
HALO = 8
BLOCK = TILE + 2 * HALO
GROUP = 8
BEAMS = 256
LANES = 128
TAPS = 4
SHIFT = 2
TILES = (4, 8, 16, 32)
FIRST = (0, 4, 12, 28)
ROWS = (48, 40, 40, 32)
BASE = (-6, -4, -2, 0)
BAND_ROWS = 96
MARGINS = ((4, 2, 6, 0), (1, 7, 3, 5))
STEPS = (3, 5, 1, 7, 2, 6)


def build_tables(z, q, idx, shf, wts, base, slope, band, cos_t, sin_t, sections):
    origin_row = q * STRIP + z * TILE
    iota8 = lax.broadcasted_iota(jnp.int32, (8, LANES), 0)
    iota_k = lax.broadcasted_iota(jnp.int32, (BAND_ROWS, LANES), 0)

    def one(section, child, tile, origin, offset):
        cols = pl.ds(pl.multiple_of(tile * LANES, LANES), LANES)
        band[child, tile] = jnp.zeros((BEAMS, LANES), BF16)
        first = idx[child : child + 1, cols] - (origin + offset)
        weights = wts[child, :, cols].astype(F32)
        patch = jnp.zeros((BAND_ROWS, LANES), F32)
        for tap in range(TAPS):
            patch = jnp.where(iota_k == first + tap, weights[tap : tap + 1, :], patch)
        if not isinstance(offset, int):
            offset = pl.multiple_of(offset, 16)
        band[child, tile, pl.ds(offset, BAND_ROWS), :] = patch.astype(BF16)
        rate = slope[child : child + 1, cols]
        rows = (iota8 + (origin_row + BASE[section])).astype(F32)
        theta = base[child : child + 1, cols] + rate * rows
        c, s = jnp.cos(theta), jnp.sin(theta)
        turn = jnp.broadcast_to(rate * 8.0, (8, LANES))
        c8, s8 = jnp.cos(turn), jnp.sin(turn)
        for step in range(ROWS[section] // 8):
            cos_t[child, tile, step * 8 : step * 8 + 8, :] = c
            sin_t[child, tile, step * 8 : step * 8 + 8, :] = s
            c, s = c * c8 - s * s8, s * c8 + c * s8

    for child in range(2 if 0 in sections else 0):
        for tile in range(TILES[0]):
            one(0, child, tile, 0, (0, 48, 112, 160)[tile])
    for section in sections:
        if section == 0:
            continue
        tiles = TILES[section]

        def body(tile, carry, section=section, tiles=tiles):
            block = (tile + 1) // 2
            side = (tile + 1) % 2
            for child in range(2):
                one(section, child, FIRST[section] + tile, LANES * (block - 1), 48 + 64 * side)
            return carry

        lax.fori_loop(0, tiles, body, 0)


def masks_of(shf, tile):
    found = []
    for child in range(2):
        cols = pl.ds(pl.multiple_of(tile * LANES, LANES), LANES)
        row = jnp.broadcast_to(shf[child : child + 1, cols], (16, LANES))
        found.append({o: row == o for o in (-2, -1, 1, 2)})
    return found


def pieces_of(section, part):
    if part == 1:
        low, high = (0, 24) if section == 3 else (32, 56)
        return (
            (2, 0, 8, ((low, 0, 8, 8),)),
            (22, 36 - 4 * section, 8, ((high, 0, 8, 8),)),
        )
    if section == 3:
        return ((2, 8, 16, ((8, 0, 8, 8), (16, 8, 8, 8))),)
    start = (2, 8, 16, ((0, 0, 16, 16), (40, 0, 8, 8)))
    if section == 0:
        return (start, (18, 24, 16, ((16, 0, 16, 16),)), (22, 28, 8, ((48, 0, 8, 8),)))
    if section == 1:
        return (start, (18, 24, 8, ((16, 0, 8, 16), (48, 0, 8, 8))))
    return (start, (18, 24, 8, ((16, 0, 8, 16),)), (14, 20, 8, ((48, 0, 8, 8),)))


def combine(section, part, row0, v, slot, masks, cos_t, sin_t, tile, store):
    for at, phase, count, places in pieces_of(section, part):
        moved = []
        for child in range(2):
            for plane in range(2):
                u = v[(*slot, child, plane, slice(at, at + count), slice(None))]
                for o in (-2, -1, 1, 2):
                    other = v[(*slot, child, plane, slice(at + o, at + o + count), slice(None))]
                    u = jnp.where(masks[child][o][:count], other, u)
                moved.append(u)
        rows = slice(phase, phase + count)
        c0, s0 = cos_t[0, tile, rows, :], sin_t[0, tile, rows, :]
        c1, s1 = cos_t[1, tile, rows, :], sin_t[1, tile, rows, :]
        parts = [
            (c0 * moved[0] - s0 * moved[1]) + (c1 * moved[2] - s1 * moved[3]),
            (s0 * moved[0] + c0 * moved[1]) + (s1 * moved[2] + c1 * moved[3]),
        ]
        if part == 1 and section < 3:
            bins = lax.broadcasted_iota(jnp.int32, (count, LANES), 0)
            bins = bins + (row0 + phase + BASE[section])
            inside = (bins >= 0) & (bins < STRIPS * STRIP)
            parts = [jnp.where(inside, value, 0.0) for value in parts]
        for to, first, taken, written in places:
            for plane in range(2):
                value = parts[plane][first : first + taken]
                if written > taken:
                    rest = jnp.zeros((written - taken, LANES), F32)
                    value = jnp.concatenate([value, rest], axis=0)
                store(plane, slice(to, to + written), value.astype(BF16))


def section_zero(images, part, row0, recv, shf, band, cos_t, sin_t, v, out):
    def slot_of(k, t):
        return (k // 2, (k % 2) * 4 + t)

    for k, image in enumerate(images):
        for child in range(2):
            if part == 0:
                lhs = recv[image, :, child, 1:5].reshape(2 * 32, BEAMS)
            else:
                ends = [recv[image, :, child, at : at + 2].reshape(2, 16, BEAMS) for at in (0, 4)]
                lhs = jnp.concatenate(ends, axis=1).reshape(2 * 32, BEAMS)
            rhs = jnp.concatenate([band[child, t] for t in range(4)], axis=1)
            product = jnp.dot(lhs, rhs, preferred_element_type=F32)
            for plane in range(2):
                for t in range(4):
                    v[(*slot_of(k, t), child, plane, slice(0, 32), slice(None))] = product[
                        plane * 32 : (plane + 1) * 32, t * LANES : (t + 1) * LANES
                    ]
    for t in range(4):
        masks = masks_of(shf, t)
        for k, image in enumerate(images):

            def store(plane, rows, value, t=t, image=image):
                out[plane, image, rows, t * LANES : (t + 1) * LANES] = value

            combine(0, part, row0, v, slot_of(k, t), masks, cos_t, sin_t, t, store)


def section_later(section, part, chosen, row0, source, shf, band, cos_t, sin_t, v, out):
    images = 8 >> section
    tiles = TILES[section]
    rows = 32
    half = slice(part * 32, part * 32 + rows)

    blocks = tiles // 2

    def tiles_of(block):
        return ((2 * block - 1) % tiles, 2 * block)

    def slot_of(block, image, side):
        n = (block * len(chosen) + image) * 2 + side
        return (n // 8, n % 8)

    def multiply(block):
        here = tiles_of(block)
        for child in range(2):
            lhs = jnp.concatenate(
                [
                    jnp.concatenate(
                        [
                            source[:, child * images + image, half, t * LANES : (t + 1) * LANES]
                            for t in ((block - 1) % blocks, block)
                        ],
                        axis=2,
                    )
                    for image in chosen
                ],
                axis=1,
            ).reshape(2 * len(chosen) * rows, BEAMS)
            rhs = jnp.concatenate([band[child, FIRST[section] + t] for t in here], axis=1)
            product = jnp.dot(lhs, rhs, preferred_element_type=F32)
            for plane in range(2):
                for image in range(len(chosen)):
                    at = (plane * len(chosen) + image) * rows
                    for side in range(2):
                        to = (*slot_of(block, image, side), child, plane, slice(0, rows), slice(None))
                        v[to] = product[at : at + rows, side * LANES : (side + 1) * LANES]

    def finish(block):
        for side, t in enumerate(tiles_of(block)):
            tile = FIRST[section] + t
            masks = masks_of(shf, tile)
            cols = slice(t * LANES, (t + 1) * LANES)
            for k, image in enumerate(chosen):

                def store(plane, rows, value, cols=cols, image=image):
                    if section == 3:
                        out[plane, rows, cols] = value
                    else:
                        out[plane, image, rows, cols] = value

                slots = slot_of(block, k, side)
                combine(section, part, row0, v, slots, masks, cos_t, sin_t, tile, store)

    order = [*range(1, blocks), 0]
    multiply(order[0])
    for now, later in zip(order, order[1:]):
        multiply(later)
        finish(now)
    finish(order[-1])


def kernel(
    images, idx_h, shf_h, wts_h, base_h, slope_h, final,
    recv, relay, idx, shf, wts, base, slope, band, cos_t, sin_t, s1, s2, s3, v0, v1, v2, v3,
    local_sem, table_sem, send_sem, recv_sem, relay_sem, forward_sem, margin_sem, edge_sem, comm=True, place=None,
):
    if comm:
        sub, q = lax.axis_index("sub"), lax.axis_index("rng")
        z, lane = sub // COLUMN, sub % COLUMN
    else:
        z, q = jnp.int32(place[0]), jnp.int32(place[1])

    def device(zz, qq):
        return (zz * COLUMN + lane, qq)

    groups = TILE // GROUP
    has_next = (z < CHIPS - 1) | (q < STRIPS - 1)
    has_previous = (z > 0) | (q > 0)

    def beside(side):
        if side == 0:
            return device((z + 1) % CHIPS, q + (z == CHIPS - 1).astype(jnp.int32))
        return device((z + CHIPS - 1) % CHIPS, q - (z == 0).astype(jnp.int32))

    if comm:
        barrier = pltpu.get_barrier_semaphore()
        for step in range(1, CHIPS):
            pl.semaphore_signal(
                barrier, inc=1, device_id=device((z + step) % CHIPS, q), device_id_type=MESH
            )
        leaves_up = (z == CHIPS - 1) & (q < STRIPS - 1)
        leaves_down = (z == 0) & (q > 0)

        @pl.when(leaves_up)
        def _():
            pl.semaphore_signal(barrier, inc=1, device_id=beside(0), device_id_type=MESH)

        @pl.when(leaves_down)
        def _():
            for other in range(CHIPS):
                pl.semaphore_signal(
                    barrier, inc=1, device_id=device(other, q - 1), device_id_type=MESH
                )

    fetches = [
        pltpu.make_async_copy(src, dst, table_sem.at[i])
        for i, (src, dst) in enumerate(
            ((idx_h, idx), (shf_h, shf), (wts_h, wts), (base_h, base), (slope_h, slope))
        )
    ]
    for fetch in fetches:
        fetch.start()

    main = pl.ds(1, groups)

    def of_tile(to, first=0, count=groups):
        return pl.ds(to * groups + first, count)

    if comm:
        own = pltpu.make_async_copy(
            images.at[:, :, of_tile(z)], recv.at[z, :, :, main], local_sem
        )
        own.start()
        below = q < STRIPS - 1
        peers = CHIPS - 1 + below.astype(jnp.int32) + leaves_down.astype(jnp.int32)
        pl.semaphore_wait(barrier, peers)

        def block_copy(step):
            to = (z + step) % CHIPS
            return pltpu.make_async_remote_copy(
                src_ref=images.at[:, :, of_tile(to)],
                dst_ref=recv.at[z, :, :, main],
                send_sem=send_sem.at[step],
                recv_sem=recv_sem.at[step],
                device_id=device(to, q),
                device_id_type=MESH,
            )

        def relay_copy(way):
            return pltpu.make_async_remote_copy(
                src_ref=images.at[:, :, of_tile((z + 4) % CHIPS, 2 * way, 2)],
                dst_ref=relay.at[way],
                send_sem=relay_sem.at[0, way],
                recv_sem=relay_sem.at[1, way],
                device_id=device((z + (2, 6)[way]) % CHIPS, q),
                device_id_type=MESH,
            )

        def forward_copy(way):
            return pltpu.make_async_remote_copy(
                src_ref=relay.at[way],
                dst_ref=recv.at[(z + (6, 2)[way]) % CHIPS, :, :, pl.ds(1 + 2 * way, 2)],
                send_sem=forward_sem.at[0, way],
                recv_sem=forward_sem.at[1, way],
                device_id=device((z + (2, 6)[way]) % CHIPS, q),
                device_id_type=MESH,
            )

        def margin_copy(side, image):
            return pltpu.make_async_remote_copy(
                src_ref=recv.at[image, :, :, (groups, 1)[side]],
                dst_ref=recv.at[image, :, :, (0, groups + 1)[side]],
                send_sem=margin_sem.at[0, side, image],
                recv_sem=margin_sem.at[1, side, image],
                device_id=beside(side),
                device_id_type=MESH,
            )

        def edge_copy():
            return pltpu.make_async_remote_copy(
                src_ref=images.at[:, :, STRIP // GROUP - 1],
                dst_ref=recv.at[z, :, :, 0],
                send_sem=edge_sem,
                recv_sem=margin_sem.at[1, 0, z],
                device_id=device(0, q + 1),
                device_id_type=MESH,
            )

        @pl.when(below)
        def _():
            edge_copy().start()

        for way in range(2):
            relay_copy(way).start()
        for step in STEPS:
            block_copy(step).start()

        @pl.when(jnp.logical_not(has_previous))
        def _():
            recv[:, :, :, 0] = jnp.zeros((CHIPS, 2, 2, GROUP, BEAMS), BF16)

        @pl.when(jnp.logical_not(has_next))
        def _():
            recv[:, :, :, groups + 1] = jnp.zeros((CHIPS, 2, 2, GROUP, BEAMS), BF16)
    else:
        own = pltpu.make_async_copy(images, recv, local_sem)
        own.start()

    for fetch in fetches:
        fetch.wait()
    tables = (z, q, idx, shf, wts, base, slope, band, cos_t, sin_t)
    build_tables(*tables, sections=(0, 1, 2))
    if comm:
        for way in range(2):
            relay_copy(way).wait_recv()
            forward_copy(way).start()
    build_tables(*tables, sections=(3,))
    own.wait()
    row0 = q * STRIP + z * TILE

    def arrival(turn, carry):
        step = jnp.int32(0)
        for position, distance in enumerate((*STEPS, 4)):
            step = jnp.where(turn == position + 1, distance, step)
        image = (z + CHIPS - step) % CHIPS
        if comm:

            @pl.when((turn > 0) & (turn < CHIPS - 1))
            def _():
                block_copy(step).wait_recv()

            @pl.when(turn == CHIPS - 1)
            def _():
                for way in range(2):
                    forward_copy(way).wait_recv()

            for side, there in ((1, has_previous), (0, z < CHIPS - 1)):

                @pl.when(there)
                def _(side=side):
                    margin_copy(side, image).start()

        section_zero([image], 0, row0, recv, shf, band, cos_t, sin_t, v0, s1)
        return carry

    def outer(images):
        if comm:
            for image in images:

                @pl.when(has_previous)
                def _(image=image):
                    margin_copy(0, image).wait_recv()

                @pl.when(has_next)
                def _(image=image):
                    margin_copy(1, image).wait_recv()

        section_zero(images, 1, row0, recv, shf, band, cos_t, sin_t, v0, s1)

    def merge(section, part, chosen):
        source, v, out = ((s1, v1, s2), (s2, v2, s3), (s3, v3, final))[section - 1]
        section_later(section, part, chosen, row0, source, shf, band, cos_t, sin_t, v, out)

    lax.fori_loop(0, 5, arrival, 0)
    merge(1, 0, [(z + 7) % 4, (z + 5) % 4])
    merge(2, 0, [(z + 7) % 2])
    lax.fori_loop(5, 7, arrival, 0)
    merge(1, 0, [(z + 6) % 4])
    lax.fori_loop(7, 8, arrival, 0)
    merge(1, 0, [z % 4])
    merge(2, 0, [z % 2])
    merge(3, 0, [0])
    for turn in MARGINS:
        outer([(z + CHIPS - step) % CHIPS for step in turn])
    for section in range(1, 4):
        merge(section, 1, list(range(8 >> section)))

    if comm:
        for way in range(2):
            relay_copy(way).wait_send()
            forward_copy(way).wait_send()
        for step in STEPS:
            block_copy(step).wait_send()
        for side, there in ((1, has_previous), (0, z < CHIPS - 1)):

            @pl.when(there)
            def _(side=side):
                for image in range(CHIPS):
                    margin_copy(side, image).wait_send()

        @pl.when(below)
        def _():
            edge_copy().wait_send()


def call(images, tables, comm=True, place=None):
    vmem = pl.BlockSpec(memory_space=pltpu.VMEM)
    hbm = pl.BlockSpec(memory_space=pltpu.HBM)
    dma = pltpu.SemaphoreType.DMA
    tiles = sum(TILES)
    params = dict(vmem_limit_bytes=48 * 2**20, has_side_effects=True)
    if comm:
        params["collective_id"] = 0
    return pl.pallas_call(
        functools.partial(kernel, comm=comm, place=place),
        out_shape=jax.ShapeDtypeStruct((2, TILE, 4096), BF16),
        in_specs=[hbm] * 6,
        out_specs=vmem,
        scratch_shapes=[
            pltpu.VMEM((CHIPS, 2, 2, BLOCK // GROUP, GROUP, BEAMS), BF16),
            pltpu.VMEM((2, 2, 2, 2, GROUP, BEAMS), BF16),
            *[pltpu.VMEM(table.shape, table.dtype) for table in tables],
            pltpu.VMEM((2, tiles, BEAMS, LANES), BF16),
            pltpu.VMEM((2, tiles, BLOCK, LANES), F32),
            pltpu.VMEM((2, tiles, BLOCK, LANES), F32),
            pltpu.VMEM((2, 8, 64, 512), BF16),
            pltpu.VMEM((2, 4, 64, 1024), BF16),
            pltpu.VMEM((2, 2, 64, 2048), BF16),
            *[pltpu.VMEM((4, 8, 2, 2, count, LANES), F32) for count in (40, 40, 40, 40)],
            dma,
            dma((len(tables),)),
            dma((CHIPS,)),
            dma((CHIPS,)),
            dma((2, 2)),
            dma((2, 2)),
            dma((2, 2, CHIPS)),
            dma,
        ],
        compiler_params=pltpu.CompilerParams(**params),
    )(images, *tables)


def local(images, *tables):
    grouped = images.reshape(2, 2, STRIP // GROUP, GROUP, BEAMS)
    grouped, *tables = (pltpu.with_memory_space_constraint(x, pltpu.HBM) for x in (grouped, *tables))
    return call(grouped, tables).reshape(2, 1, 1, TILE, 4096)


def solution(mesh):
    in_specs = (P(None, "sub", "rng", None), P(), P(), P(), P(), P())
    out_specs = P(None, "sub", "rng", None, None)
    return jax.shard_map(local, mesh=mesh, in_specs=in_specs, out_specs=out_specs, check_vma=False)
```
